128 devices in a mesh: row: 16 (over z, y_lo, core), col: 8 (over x, y_hi).
Axes of the slice: x: 4, y: 4 (y_hi: 2, y_lo: 2; y = y_hi * 2 + y_lo), z: 4, core: 2. Of those that a mesh axis runs over, the one named last changes fastest.
Arguments:
- image: bfloat16 [128, 1024, 768], P('row', 'col'), may hold values from -6 to 6
- skip_rows: bfloat16 [131072, 768], P(('row', 'col')), may hold values from -6 to 6
- owners: int32 [131072, 1], P(('row', 'col')), may hold values from 0 to 127, as said below
- positions: int32 [131072], P(('row', 'col')), may hold values from 0 to 1023, as said below
- gain: float32 [768], replicated, may hold values from 0.5 to 1.5
- w_qkv: bfloat16 [768, 2304], replicated, may hold values from -0.21875 to 0.21875
- w_out: bfloat16 [768, 768], replicated, may hold values from -0.4375 to 0.4375
- head_scale: float32 [12], replicated, may hold values from 4 to 300
Outputs:
- level_out: bfloat16 [128, 1024, 768], P('row', 'col')
The draws below stay inside these ranges and needn't reach their ends.
Inputs may be any that keep to these rules, and one draw needn't show every extreme that they name: `owners`: at most 16 of the 1024 rows of one device name one owner, and some device sends exactly 16 rows to some owner; every owner is named by exactly 1024 rows in all. The pairs (owners, positions) name every cell of the image exactly once.
All inputs are finite; a program needn't handle non-finite values.
Results may differ from the reference program's by a relative error of at most 0.017.
The reference program's roundings to bfloat16 on the way (of `normed`, `keyval`, `query_unit`, `key_unit`, `weights` and `attended`) count: a program that leaves them out, or rounds other values in their place, can miss the bound.
Values may be sent and summed in bfloat16 or wider, within the bound.
A program may use at most 128 MiB of HBM per device.

```python
import jax
import jax.numpy as jnp
from jax import lax

HEADS = 12
HEAD_DIM = 64
D = 768
TH = 8
TW = 128
R_DEV = 1024
CAP = 16
IMG_ROWS = 128
IMG_COLS = 1024
SOURCE_ROWS = 131072
N_COL = 8
DEVICES = 128


def placement_tables(key):
    half_count = DEVICES // 2
    levels = jax.random.randint(jax.random.fold_in(key, 11), (half_count,), 0, 5).astype(jnp.int32)
    levels = levels.at[0].set(4)
    first_share = levels * (CAP // 4)
    by_gap = jnp.concatenate([first_share, CAP - first_share])
    by_gap = by_gap[jax.random.permutation(jax.random.fold_in(key, 12), DEVICES)]
    sources = jnp.arange(DEVICES, dtype=jnp.int32)
    counts = by_gap[(sources[None, :] - sources[:, None]) % DEVICES]
    starts = jnp.cumsum(counts, axis=0) - counts
    offsets = jnp.cumsum(counts, axis=1) - counts

    def one_source(count_row, offset_row, source_key):
        owner_seq = jnp.repeat(sources, count_row, total_repeat_length=R_DEV)
        rank_seq = jnp.arange(R_DEV, dtype=jnp.int32) - offset_row[owner_seq]
        shuffle = jax.random.permutation(source_key, R_DEV)
        return (owner_seq[shuffle], rank_seq[shuffle])

    def one_owner(owner_key):
        return jax.random.permutation(owner_key, R_DEV).astype(jnp.int32)
    row_keys = jax.random.split(jax.random.fold_in(key, 13), DEVICES)
    owner_table, rank_table = jax.vmap(one_source)(counts, offsets, row_keys)
    cell_keys = jax.random.split(jax.random.fold_in(key, 14), DEVICES)
    cell_perm = jax.vmap(one_owner)(cell_keys)
    slot_index = starts[sources[:, None], owner_table] + rank_table
    cell_ids = cell_perm[owner_table, slot_index]
    return (owner_table.reshape(-1).astype(jnp.int32), cell_ids.reshape(-1).astype(jnp.int32))


def draw_owners(key, part):
    owner_table, cell_ids = placement_tables(key)
    return owner_table.reshape(-1, 1)


def draw_positions(key, part):
    owner_table, cell_ids = placement_tables(key)
    return cell_ids


def draw_head_scale(key, part):
    key = jax.random.fold_in(key, 5)
    uniform_draw = jax.random.uniform(key, (HEADS,), jnp.float32)
    return 4.0 * jnp.exp(uniform_draw * jnp.log(4.0))


def block_scale(stream_key, extent, pieces, low, largest):
    def one(axis_at, blocks):
        steps = jax.random.uniform(jax.random.fold_in(jax.random.fold_in(stream_key, 6), axis_at), (blocks,), jnp.float32, low / len(pieces), largest / len(pieces))
        return jnp.repeat(jnp.exp(steps), extent[axis_at] // blocks).reshape((-1,) + (1,) * (len(extent) - axis_at - 1))

    factor_of = one(*pieces[0])
    for cut in pieces[1:]:
        factor_of = factor_of * one(*cut)
    return factor_of


def centred(own_key, extent, spread, reach, cuts=(), held_as=jnp.bfloat16):
    values = spread * jax.random.normal(own_key, extent, jnp.float32)
    if cuts:
        values = values * block_scale(own_key, extent, cuts, -0.22, 0.18)
    return jnp.clip(values, -reach, reach).astype(held_as)


def setup_inputs(seed: int = 0) -> dict:
    keys = jax.random.split(jax.random.key(seed), 9)
    return {
        "image": centred(keys[0], (IMG_ROWS, IMG_COLS, D), 1.0, 6.0, ((0, 16), (1, 8))),
        "skip_rows": centred(keys[1], (SOURCE_ROWS, D), 1.0, 6.0, ((0, 128),)),
        "owners": draw_owners(jax.random.fold_in(keys[8], 71), 0),
        "positions": draw_positions(jax.random.fold_in(keys[8], 71), 0),
        "gain": jnp.clip(1.0 + 0.1 * jax.random.normal(keys[4], (D,), jnp.float32), 0.5, 1.5),
        "w_qkv": centred(keys[5], (D, 3 * D), D ** -0.5, 0.21875),
        "w_out": centred(keys[6], (D, D), (D // 4) ** -0.5, 0.4375),
        "head_scale": draw_head_scale(jax.random.fold_in(keys[8], 71), 0),
    }


def reference(image, skip_rows, owners, positions, gain, w_qkv, w_out, head_scale):
    rim_width = 3
    image_rows, image_cols, model_width = image.shape
    owner_ids = owners[:, 0]
    global_row = owner_ids // N_COL * TH + positions // TW
    global_col = owner_ids % N_COL * TW + positions % TW
    skip = jnp.zeros((image_rows, image_cols, model_width), jnp.float32)
    skip = skip.at[global_row, global_col].add(skip_rows.astype(jnp.float32))
    resid = image.astype(jnp.float32) + skip
    normed = (resid * lax.rsqrt(lax.optimization_barrier(jnp.mean(resid * resid, axis=-1, keepdims=True)) + 1e-06) * gain).astype(jnp.bfloat16)
    flat_rows = normed.reshape(-1, model_width)
    queries = jnp.dot(flat_rows, w_qkv[:, :model_width], preferred_element_type=jnp.float32)
    queries = queries.reshape(image_rows, image_cols, HEADS, HEAD_DIM)
    keyval = jnp.dot(flat_rows, w_qkv[:, model_width:], preferred_element_type=jnp.float32).astype(jnp.bfloat16)
    keyval = keyval.reshape(image_rows, image_cols, 2, HEADS, HEAD_DIM)
    query_unit = (queries * head_scale[:, None] * lax.rsqrt(lax.optimization_barrier(jnp.sum(queries * queries, axis=-1, keepdims=True)) + 1e-06)).astype(jnp.bfloat16)
    keys_raw = keyval[:, :, 0].astype(jnp.float32)
    key_unit = (keys_raw * lax.rsqrt(lax.optimization_barrier(jnp.sum(keys_raw * keys_raw, axis=-1, keepdims=True)) + 1e-06)).astype(jnp.bfloat16)
    values = keyval[:, :, 1]
    padding = ((rim_width, rim_width), (rim_width, rim_width), (0, 0), (0, 0))
    key_padded = jnp.pad(key_unit, padding)
    value_padded = jnp.pad(values, padding)
    row_range = jnp.arange(image_rows, dtype=jnp.int32)
    col_range = jnp.arange(image_cols, dtype=jnp.int32)
    query_float = query_unit.astype(jnp.float32)
    zero_index = jnp.zeros((), jnp.int32)

    def score_step(carry, offset):
        off_row = offset // 7
        off_col = offset % 7
        shifted = lax.dynamic_slice(key_padded, (off_row, off_col, zero_index, zero_index), (image_rows, image_cols, HEADS, HEAD_DIM))
        score_map = lax.optimization_barrier(jnp.sum(query_float * shifted.astype(jnp.float32), axis=-1))
        row_ok = (row_range + off_row - rim_width >= 0) & (row_range + off_row - rim_width < image_rows)
        col_ok = (col_range + off_col - rim_width >= 0) & (col_range + off_col - rim_width < image_cols)
        inside = row_ok[:, None] & col_ok[None, :]
        return (carry, jnp.where(inside[:, :, None], score_map, -1e+30))
    offsets = jnp.arange(49, dtype=jnp.int32)
    _, scores = lax.scan(score_step, 0, offsets)
    row_max = lax.optimization_barrier(jnp.max(scores, axis=0, keepdims=True))
    expo_terms = jnp.exp(scores - row_max)
    probs = expo_terms / lax.optimization_barrier(jnp.sum(expo_terms, axis=0, keepdims=True))
    weights = probs.astype(jnp.bfloat16)

    def mix_step(running, inputs):
        offset, weight_map = inputs
        off_row = offset // 7
        off_col = offset % 7
        shifted = lax.dynamic_slice(value_padded, (off_row, off_col, zero_index, zero_index), (image_rows, image_cols, HEADS, HEAD_DIM))
        return (running + weight_map.astype(jnp.float32)[..., None] * shifted.astype(jnp.float32), None)
    start = jnp.zeros((image_rows, image_cols, HEADS, HEAD_DIM), jnp.float32)
    attended, _ = lax.scan(mix_step, start, (offsets, weights))
    attended = attended.astype(jnp.bfloat16).reshape(-1, model_width)
    projected = jnp.dot(attended, w_out, preferred_element_type=jnp.float32).reshape(image_rows, image_cols, model_width)
    return (resid + projected).astype(jnp.bfloat16)
```

```python
import functools

import jax
import jax.numpy as jnp
from jax import lax
from jax.experimental import pallas as pl
from jax.experimental.pallas import tpu as pltpu
from jax.sharding import PartitionSpec as P

RIM = 3
PAD = 8
GROUP_ROWS = 4
GROUP_COLS = 16
HEAD = 64
QUAD = 256


def dot(a, b):
    return jnp.dot(a, b, preferred_element_type=jnp.float32)


def dot_nt(a, b):
    return lax.dot_general(a, b, (((1,), (1,)), ((), ())), preferred_element_type=jnp.float32)


def head_sums(x, ones):
    square = x * x
    high = square.astype(jnp.bfloat16)
    low = (square - high.astype(jnp.float32)).astype(jnp.bfloat16)
    width = x.shape[1]
    parts = []
    for start in range(0, width, QUAD):
        lanes = slice(start, start + QUAD)
        parts.append(dot(high[:, lanes], ones) + dot(low[:, lanes], ones))
    return jnp.concatenate(parts, axis=1)


def attend_kernel(
    normed_ref, skip_ref, image_ref, w_qkv_ref, w_out_ref, scale_ref, out_ref,
    query_s, key_s, value_s, attended_s,
):
    ext_rows, ext_cols, width = normed_ref.shape
    tile_rows, tile_cols, _ = image_ref.shape
    image_rows = tile_rows * lax.axis_size("row")
    image_cols = tile_cols * lax.axis_size("col")
    row_base = lax.axis_index("row") * tile_rows
    col_base = lax.axis_index("col") * tile_cols
    lane_a = lax.broadcasted_iota(jnp.int32, (QUAD, QUAD), 0) // HEAD
    lane_b = lax.broadcasted_iota(jnp.int32, (QUAD, QUAD), 1) // HEAD
    ones = (lane_a == lane_b).astype(jnp.float32).astype(jnp.bfloat16)

    def keyval_step(step, carry):
        x = normed_ref[pl.ds(step * 2, 2)].reshape(2 * ext_cols, width)
        keys = dot(x, w_qkv_ref[:, width : 2 * width]).astype(jnp.bfloat16)
        keys = keys.astype(jnp.float32)
        unit = keys * lax.rsqrt(head_sums(keys, ones) + 1e-06)
        key_s[pl.ds(step * 2, 2)] = unit.astype(jnp.bfloat16).reshape(2, ext_cols, width)
        values = dot(x, w_qkv_ref[:, 2 * width :])
        value_s[pl.ds(step * 2, 2)] = values.astype(jnp.bfloat16).reshape(2, ext_cols, width)
        return carry

    lax.fori_loop(0, ext_rows // 2, keyval_step, 0)

    def query_step(step, carry):
        x = normed_ref[pl.ds(step * 2 + RIM, 2), PAD : PAD + tile_cols]
        queries = dot(x.reshape(2 * tile_cols, width), w_qkv_ref[:, :width])
        unit = queries * scale_ref[...] * lax.rsqrt(head_sums(queries, ones) + 1e-06)
        query_s[pl.ds(step * 2, 2)] = unit.astype(jnp.bfloat16).reshape(2, tile_cols, width)
        return carry

    lax.fori_loop(0, tile_rows // 2, query_step, 0)

    key_rows = GROUP_ROWS + 2 * RIM
    key_cols = GROUP_COLS + 2 * PAD
    n_query = GROUP_ROWS * GROUP_COLS
    n_key = key_rows * key_cols
    col_groups = tile_cols // GROUP_COLS
    query_at = lax.broadcasted_iota(jnp.int32, (n_query, n_key), 0)
    key_at = lax.broadcasted_iota(jnp.int32, (n_query, n_key), 1)
    row_gap = key_at // key_cols - query_at // GROUP_COLS
    col_gap = key_at % key_cols - query_at % GROUP_COLS
    near = (
        (row_gap >= 0)
        & (row_gap <= 2 * RIM)
        & (col_gap >= PAD - RIM)
        & (col_gap <= PAD + RIM)
    )
    lane_head = lax.broadcasted_iota(jnp.int32, (1, QUAD), 1) // HEAD
    heads = QUAD // HEAD

    def attend_step(step, carry):
        row_at = (step // col_groups) * GROUP_ROWS
        col_at = pl.multiple_of((step % col_groups) * GROUP_COLS, GROUP_COLS)
        key_row = row_base + row_at - RIM + key_at // key_cols
        key_col = col_base + col_at - PAD + key_at % key_cols
        inside = (
            near & (key_row >= 0) & (key_row < image_rows) & (key_col >= 0) & (key_col < image_cols)
        )
        bias = jnp.where(inside, 0.0, -1e30)
        for start in range(0, width, QUAD):
            lanes = slice(start, start + QUAD)
            query = query_s[pl.ds(row_at, GROUP_ROWS), pl.ds(col_at, GROUP_COLS), lanes]
            query = query.reshape(n_query, QUAD)
            keys = key_s[pl.ds(row_at, key_rows), pl.ds(col_at, key_cols), lanes]
            keys = keys.reshape(n_key, QUAD)
            values = value_s[pl.ds(row_at, key_rows), pl.ds(col_at, key_cols), lanes]
            values = values.reshape(n_key, QUAD)
            spread = jnp.concatenate(
                [
                    query * (lane_head == h).astype(jnp.float32).astype(jnp.bfloat16)
                    for h in range(heads)
                ],
                axis=0,
            )
            scores = dot_nt(spread, keys)
            scores = (scores.reshape(heads, n_query, n_key) + bias[None]).reshape(-1, n_key)
            top = jnp.max(scores, axis=1, keepdims=True)
            expo = jnp.exp(scores - top)
            inverse = 1.0 / jnp.sum(expo, axis=1, keepdims=True)
            mixed = dot((expo * inverse).astype(jnp.bfloat16), values)
            joined = mixed[:n_query]
            for h in range(1, heads):
                part = mixed[h * n_query : (h + 1) * n_query]
                joined = jnp.where(lane_head == h, part, joined)
            attended_s[pl.ds(row_at, GROUP_ROWS), pl.ds(col_at, GROUP_COLS), lanes] = (
                joined.astype(jnp.bfloat16).reshape(GROUP_ROWS, GROUP_COLS, QUAD)
            )
        return carry

    lax.fori_loop(0, (tile_rows // GROUP_ROWS) * col_groups, attend_step, 0)

    def out_step(step, carry):
        rows = pl.ds(step * 2, 2)
        resid = image_ref[rows].astype(jnp.float32) + skip_ref[rows].astype(jnp.float32)
        projected = dot(attended_s[rows].reshape(2 * tile_cols, width), w_out_ref[...])
        out_ref[rows] = (resid + projected.reshape(2, tile_cols, width)).astype(jnp.bfloat16)
        return carry

    lax.fori_loop(0, tile_rows // 2, out_step, 0)


def attend(normed, skip, image, w_qkv, w_out, scale):
    tile_rows, tile_cols, width = image.shape
    vmem = pl.BlockSpec(memory_space=pltpu.VMEM)
    return pl.pallas_call(
        attend_kernel,
        out_shape=jax.ShapeDtypeStruct(image.shape, jnp.bfloat16),
        in_specs=[vmem] * 6,
        out_specs=vmem,
        scratch_shapes=[
            pltpu.VMEM(image.shape, jnp.bfloat16),
            pltpu.VMEM(normed.shape, jnp.bfloat16),
            pltpu.VMEM(normed.shape, jnp.bfloat16),
            pltpu.VMEM(image.shape, jnp.bfloat16),
        ],
        compiler_params=pltpu.CompilerParams(vmem_limit_bytes=56 << 20),
        name="attend",
    )(normed, skip, image, w_qkv, w_out, scale)


def extended(array, axis, dim, width, pad):
    peers, length = (lax.axis_size(axis), array.shape[dim])
    up = [(i, i + 1) for i in range(peers - 1)]
    down = [(j, i) for i, j in up]
    last = lax.slice_in_dim(array, length - width, length, axis=dim)
    first = lax.slice_in_dim(array, 0, width, axis=dim)
    before = lax.ppermute(last, axis, up)
    after = lax.ppermute(first, axis, down)
    blank = list(array.shape)
    blank[dim] = pad - width
    blank = jnp.zeros(blank, array.dtype)
    return jnp.concatenate([blank, before, array, after, blank], axis=dim)


def local(image, skip_rows, owners, positions, gain, w_qkv, w_out, head_scale):
    tile_rows, tile_cols, model_width = image.shape
    device_count = lax.axis_size("row") * lax.axis_size("col")
    rows_held = skip_rows.shape[0]
    capacity = 2 * rows_held // device_count
    cell_count = tile_rows * tile_cols
    owner_ids = owners[:, 0]
    one_hot = (owner_ids[:, None] == jnp.arange(device_count, dtype=jnp.int32)[None, :]).astype(
        jnp.int32
    )
    earlier = jnp.cumsum(one_hot, axis=0) - one_hot
    row_rank = jnp.sum(earlier * one_hot, axis=1)
    slot_index = owner_ids * capacity + row_rank
    send_rows = (
        jnp.zeros((device_count * capacity, model_width), jnp.bfloat16)
        .at[slot_index]
        .set(skip_rows)
    )
    send_cells = (
        jnp.full((device_count * capacity,), cell_count, jnp.int32).at[slot_index].set(positions)
    )
    got_rows, got_cells = (
        lax.all_to_all(
            send_rows.reshape(device_count, capacity, model_width),
            ("row", "col"),
            split_axis=0,
            concat_axis=0,
            tiled=True,
        ),
        lax.all_to_all(
            send_cells.reshape(device_count, capacity),
            ("row", "col"),
            split_axis=0,
            concat_axis=0,
            tiled=True,
        ),
    )
    skip = jnp.zeros((cell_count, model_width), jnp.bfloat16)
    skip = skip.at[got_cells.reshape(-1)].set(got_rows.reshape(-1, model_width), mode="drop")
    skip = skip.reshape(tile_rows, tile_cols, model_width)
    resid = image.astype(jnp.float32) + skip.astype(jnp.float32)
    normed = (
        resid * lax.rsqrt(jnp.mean(resid * resid, axis=-1, keepdims=True) + 1e-06) * gain
    ).astype(jnp.bfloat16)
    normed = extended(normed, "row", 0, RIM, RIM)
    normed = extended(normed, "col", 1, RIM, PAD)
    scale = jnp.repeat(head_scale, HEAD)[None, :]
    return attend(normed, skip, image, w_qkv, w_out, scale)


def solution(mesh):
    in_specs = (
        P("row", "col", None),
        P(("row", "col"), None),
        P(("row", "col"), None),
        P(("row", "col")),
        P(),
        P(),
        P(),
        P(),
    )
    out_specs = P("row", "col", None)
    return jax.shard_map(local, mesh=mesh, in_specs=in_specs, out_specs=out_specs, check_vma=False)
```

```python
import functools

import jax
import jax.numpy as jnp
from jax import lax
from jax.experimental import pallas as pl
from jax.experimental.pallas import tpu as pltpu
from jax.sharding import PartitionSpec as P

RIM = 3
PAD = 8
GROUP_ROWS = 4
GROUP_COLS = 16
HEAD = 64
QUAD = 256
SLOTS = 16
STRIDE = 49
STRIDE_INVERSE = 81
MESH = pl.DeviceIdType.MESH


def dot(a, b):
    return jnp.dot(a, b, preferred_element_type=jnp.float32)


def dot_nt(a, b):
    return lax.dot_general(a, b, (((1,), (1,)), ((), ())), preferred_element_type=jnp.float32)


def head_sums(x, ones):
    square = x * x
    high = square.astype(jnp.bfloat16)
    low = (square - high.astype(jnp.float32)).astype(jnp.bfloat16)
    width = x.shape[1]
    parts = []
    for start in range(0, width, QUAD):
        lanes = slice(start, start + QUAD)
        parts.append(dot(high[:, lanes], ones) + dot(low[:, lanes], ones))
    return jnp.concatenate(parts, axis=1)


def flag(condition):
    return jnp.where(condition, 1.0, 0.0).astype(jnp.bfloat16)


def coordinates(row, col):
    return col // 2, (col % 2) * 2 + (row // 2) % 2, row // 4, row % 2


def place_kernel(
    rows_ref, owner_ref, position_ref, image_ref, gain_ref,
    own_out, skip_out, up_out, down_out, left_out, right_out,
    send_s, got_s, cell_send_s, cell_got_s, total_s, own_s, left_s, right_s,
    up_land, down_land, left_land, right_land,
    send_sem, cell_send_sem, got_sems, cell_got_sems, halo_send_sems, halo_got_sems,
):
    n_row, n_col = lax.axis_size("row"), lax.axis_size("col")
    n_device = n_row * n_col
    n_held, width = rows_ref.shape
    tile_rows, tile_cols, _ = image_ref.shape
    n_cell = tile_rows * tile_cols
    my_row, my_col = lax.axis_index("row"), lax.axis_index("col")
    my_x, my_y, my_z, my_core = coordinates(my_row, my_col)
    chunk = 16
    chunk_slots = chunk * SLOTS
    n_chunk = n_device // chunk

    def partner(step):
        gap = (step * STRIDE) % n_device
        x = (my_x + gap // 32) % 4
        y = (my_y + (gap // 8) % 4) % 4
        z = (my_z + (gap // 2) % 4) % 4
        core = (my_core + gap % 2) % 2
        return (z * 4 + (y % 2) * 2 + core, x * 2 + y // 2)

    up_land[...] = jnp.zeros_like(up_land)
    down_land[...] = jnp.zeros_like(down_land)
    left_land[...] = jnp.zeros_like(left_land)
    right_land[...] = jnp.zeros_like(right_land)

    barrier = pltpu.get_barrier_semaphore()

    def greet(step, carry):
        pl.semaphore_signal(barrier, inc=1, device_id=partner(step), device_id_type=MESH)
        return carry

    lax.fori_loop(1, n_device, greet, 0)

    owner = owner_ref[...]
    owner_row, owner_col = owner >> 3, owner & 7
    gap_x = ((owner_col >> 1) - my_x) & 3
    gap_y = ((owner_col & 1) * 2 + ((owner_row >> 1) & 1) - my_y) & 3
    gap_z = ((owner_row >> 2) - my_z) & 3
    gap_core = ((owner_row & 1) - my_core) & 1
    order = ((((gap_x * 4 + gap_y) * 4 + gap_z) * 2 + gap_core) * STRIDE_INVERSE) & (n_device - 1)
    holds = lax.broadcasted_iota(jnp.int32, (n_device, n_held), 0) == order
    holds_f = jnp.where(holds, 1.0, 0.0)
    holds_b = holds_f.astype(jnp.bfloat16)
    earlier = jnp.zeros((n_device, n_held), jnp.float32)
    for start in range(0, n_held, 256):
        at = lax.broadcasted_iota(jnp.int32, (256, n_held), 0) + start
        to = lax.broadcasted_iota(jnp.int32, (256, n_held), 1)
        earlier = earlier + dot(holds_b[:, start : start + 256], flag(at < to))
    rank = jnp.sum(earlier * holds_f, axis=0, keepdims=True).astype(jnp.int32)
    slot = order * SLOTS + rank
    code = position_ref[...] + 1
    lane = lax.broadcasted_iota(jnp.int32, (128, n_held), 0)
    parts = jnp.where(lane == rank, (code >> 5).astype(jnp.float32), 0.0)
    parts = parts + jnp.where(lane == rank + SLOTS, (code & 31).astype(jnp.float32), 0.0)
    cell_send_s[...] = dot_nt(holds_b, parts.astype(jnp.bfloat16))[:, None, :]

    total_s[...] = jnp.zeros_like(total_s)

    def row_copy(step):
        return pltpu.make_async_remote_copy(
            src_ref=send_s.at[step],
            dst_ref=got_s.at[step],
            send_sem=send_sem,
            recv_sem=got_sems.at[step // chunk],
            device_id=partner(step),
            device_id_type=MESH,
        )

    def cell_copy(step):
        return pltpu.make_async_remote_copy(
            src_ref=cell_send_s.at[step],
            dst_ref=cell_got_s.at[step],
            send_sem=cell_send_sem,
            recv_sem=cell_got_sems.at[step // chunk],
            device_id=partner(step),
            device_id_type=MESH,
        )

    def pack(index):
        at = lax.broadcasted_iota(jnp.int32, (chunk_slots, n_held), 0) + index * chunk_slots
        packed = dot(flag(at == slot), rows_ref[...])
        send_s[pl.ds(index * chunk, chunk)] = packed.astype(jnp.bfloat16).reshape(
            chunk, SLOTS, width
        )

    def send(step, carry):
        cell_copy(step).start()
        row_copy(step).start()
        return carry

    pack(0)
    pl.semaphore_wait(barrier, n_device - 1)
    pltpu.make_async_copy(send_s.at[0], got_s.at[0], got_sems.at[0]).start()
    pltpu.make_async_copy(cell_send_s.at[0], cell_got_s.at[0], cell_got_sems.at[0]).start()
    lax.fori_loop(1, chunk, send, 0)

    def pack_step(index, carry):
        pack(index)
        lax.fori_loop(index * chunk, (index + 1) * chunk, send, 0)
        return carry

    lax.fori_loop(1, n_chunk, pack_step, 0)

    table_at = lax.broadcasted_iota(jnp.int32, (128, chunk_slots), 0)
    table_slot = lax.broadcasted_iota(jnp.int32, (128, chunk_slots), 1) % SLOTS
    table = jnp.where(table_at == table_slot, 32.0, 0.0)
    table = table + jnp.where(table_at == table_slot + SLOTS, 1.0, 0.0)
    table = table.astype(jnp.bfloat16)
    source_at = lax.broadcasted_iota(jnp.int32, (chunk, chunk_slots), 0)
    source_slot = lax.broadcasted_iota(jnp.int32, (chunk, chunk_slots), 1) // SLOTS

    def unpack_step(index, carry):
        blocks = pl.ds(index * chunk, chunk)
        pltpu.make_async_copy(
            cell_got_s.at[blocks], cell_got_s.at[blocks], cell_got_sems.at[index]
        ).wait()
        codes = dot(cell_got_s[blocks].reshape(chunk, 128).astype(jnp.bfloat16), table)
        code_row = jnp.sum(
            jnp.where(source_at == source_slot, codes, 0.0), axis=0, keepdims=True
        ).astype(jnp.int32)
        cell = lax.broadcasted_iota(jnp.int32, (n_cell, chunk_slots), 0) + 1
        chosen = flag(cell == code_row)
        pltpu.make_async_copy(got_s.at[blocks], got_s.at[blocks], got_sems.at[index]).wait()
        total_s[...] += dot(chosen, got_s[blocks].reshape(chunk_slots, width))
        return carry

    lax.fori_loop(0, n_chunk, unpack_step, 0)

    def norm(start, count):
        rows = slice(start * tile_cols, (start + count) * tile_cols)
        skip = total_s[rows]
        image = image_ref[start : start + count].astype(jnp.float32)
        resid = image.reshape(count * tile_cols, width) + skip
        mean = jnp.mean(resid * resid, axis=-1, keepdims=True)
        normed = resid * lax.rsqrt(mean + 1e-06) * gain_ref[...]
        normed = normed.astype(jnp.bfloat16).reshape(count, tile_cols, width)
        own_s[start : start + count] = normed
        own_out[start : start + count] = normed
        skip_out[start : start + count] = skip.astype(jnp.bfloat16).reshape(
            count, tile_cols, width
        )

    def halo(index, there, src, dst):
        return pltpu.make_async_remote_copy(
            src_ref=src,
            dst_ref=dst,
            send_sem=halo_send_sems.at[index],
            recv_sem=halo_got_sems.at[index],
            device_id=there,
            device_id_type=MESH,
        )

    has_up, has_down = my_row > 0, my_row < n_row - 1
    has_left, has_right = my_col > 0, my_col < n_col - 1
    above, below = my_row - 1, my_row + 1
    before, after = my_col - 1, my_col + 1
    side = tile_rows * PAD
    half = side // 2
    top, bottom = pl.ds(0, half), pl.ds(half, half)
    near_top, middle, near_bottom = pl.ds(0, half), pl.ds(half, side), pl.ds(half + side, half)
    moves = (
        (has_up, has_down, (above, my_col), own_s.at[pl.ds(0, RIM)], down_land),
        (has_down, has_up, (below, my_col), own_s.at[pl.ds(tile_rows - RIM, RIM)], up_land),
        (has_left, has_right, (my_row, before), left_s, right_land.at[middle]),
        (has_right, has_left, (my_row, after), right_s, left_land.at[middle]),
        (
            has_up & has_left, has_down & has_right, (above, before),
            left_s.at[top], right_land.at[near_bottom],
        ),
        (
            has_up & has_right, has_down & has_left, (above, after),
            right_s.at[top], left_land.at[near_bottom],
        ),
        (
            has_down & has_left, has_up & has_right, (below, before),
            left_s.at[bottom], right_land.at[near_top],
        ),
        (
            has_down & has_right, has_up & has_left, (below, after),
            right_s.at[bottom], left_land.at[near_top],
        ),
    )

    def start_move(index):
        sends, _, there, src, dst = moves[index]

        @pl.when(sends)
        def _():
            halo(index, there, src, dst).start()

    norm(0, RIM)
    start_move(0)
    norm(tile_rows - RIM, RIM)
    start_move(1)
    norm(RIM, tile_rows - 2 * RIM)
    first = own_s[:, 0:16].astype(jnp.float32)[:, :PAD]
    left_s[...] = first.reshape(side, width).astype(jnp.bfloat16)
    last = own_s[:, tile_cols - 16 :].astype(jnp.float32)[:, 16 - PAD :]
    right_s[...] = last.reshape(side, width).astype(jnp.bfloat16)
    for index in range(2, len(moves)):
        start_move(index)
    for index in range(len(moves)):
        sends, gets, there, src, dst = moves[index]

        @pl.when(gets)
        def _():
            halo(index, there, src, dst).wait_recv()

        @pl.when(sends)
        def _():
            halo(index, there, src, dst).wait_send()

    up_out[...] = up_land[...]
    down_out[...] = down_land[...]
    left_out[...] = left_land[...]
    right_out[...] = right_land[...]

    others = pl.ds(1, n_device - 1)
    pltpu.make_async_copy(send_s.at[others], got_s.at[others], send_sem).wait()
    pltpu.make_async_copy(cell_send_s.at[others], cell_got_s.at[others], cell_send_sem).wait()


def place(skip_rows, owner, position, image, gain):
    tile_rows, tile_cols, width = image.shape
    n_device = lax.axis_size("row") * lax.axis_size("col")
    vmem = pl.BlockSpec(memory_space=pltpu.VMEM)
    rim = (RIM, tile_cols, width)
    side = (tile_rows * PAD, width)
    sides = (2 * tile_rows * PAD, width)
    shapes = (image.shape, image.shape, rim, rim, sides, sides)
    bf16 = jnp.bfloat16
    n_chunk = n_device // 16
    return pl.pallas_call(
        place_kernel,
        out_shape=[jax.ShapeDtypeStruct(shape, bf16) for shape in shapes],
        in_specs=[vmem] * 5,
        out_specs=[vmem] * 6,
        scratch_shapes=[
            pltpu.VMEM((n_device, SLOTS, width), bf16),
            pltpu.VMEM((n_device, SLOTS, width), bf16),
            pltpu.VMEM((n_device, 1, 128), jnp.float32),
            pltpu.VMEM((n_device, 1, 128), jnp.float32),
            pltpu.VMEM((tile_rows * tile_cols, width), jnp.float32),
            pltpu.VMEM(image.shape, bf16),
            pltpu.VMEM(side, bf16),
            pltpu.VMEM(side, bf16),
            pltpu.VMEM(rim, bf16),
            pltpu.VMEM(rim, bf16),
            pltpu.VMEM(sides, bf16),
            pltpu.VMEM(sides, bf16),
            pltpu.SemaphoreType.DMA,
            pltpu.SemaphoreType.DMA,
            pltpu.SemaphoreType.DMA((n_chunk,)),
            pltpu.SemaphoreType.DMA((n_chunk,)),
            pltpu.SemaphoreType.DMA((8,)),
            pltpu.SemaphoreType.DMA((8,)),
        ],
        compiler_params=pltpu.CompilerParams(
            collective_id=0, has_side_effects=True, vmem_limit_bytes=56 << 20
        ),
        name="place",
    )(skip_rows, owner, position, image, gain)


def attend_kernel(
    own_ref, up_ref, down_ref, left_ref, right_ref, skip_ref, image_ref, w_qkv_ref, w_out_ref, scale_ref, out_ref,
    query_s, key_s, value_s, attended_s,
):
    tile_rows, tile_cols, width = image_ref.shape
    image_rows = tile_rows * lax.axis_size("row")
    image_cols = tile_cols * lax.axis_size("col")
    row_base = lax.axis_index("row") * tile_rows
    col_base = lax.axis_index("col") * tile_cols
    lane_a = lax.broadcasted_iota(jnp.int32, (QUAD, QUAD), 0) // HEAD
    lane_b = lax.broadcasted_iota(jnp.int32, (QUAD, QUAD), 1) // HEAD
    ones = (lane_a == lane_b).astype(jnp.float32).astype(jnp.bfloat16)

    own_cols = pl.ds(PAD, tile_cols)

    def keyval(x):
        keys = dot(x, w_qkv_ref[:, width : 2 * width]).astype(jnp.bfloat16)
        keys = keys.astype(jnp.float32)
        unit = keys * lax.rsqrt(head_sums(keys, ones) + 1e-06)
        values = dot(x, w_qkv_ref[:, 2 * width :])
        return unit.astype(jnp.bfloat16), values.astype(jnp.bfloat16)

    def own_step(step, carry):
        shape = (2, tile_cols, width)
        x = own_ref[pl.ds(step * 2, 2)].reshape(2 * tile_cols, width)
        unit, values = keyval(x)
        key_s[pl.ds(step * 2 + RIM, 2), own_cols] = unit.reshape(shape)
        value_s[pl.ds(step * 2 + RIM, 2), own_cols] = values.reshape(shape)
        queries = dot(x, w_qkv_ref[:, :width])
        unit = queries * scale_ref[...] * lax.rsqrt(head_sums(queries, ones) + 1e-06)
        query_s[pl.ds(step * 2, 2)] = unit.astype(jnp.bfloat16).reshape(shape)
        return carry

    lax.fori_loop(0, tile_rows // 2, own_step, 0)
    for rim_ref, at in ((up_ref, 0), (down_ref, RIM + tile_rows)):
        unit, values = keyval(rim_ref[...].reshape(RIM * tile_cols, width))
        key_s[at : at + RIM, own_cols] = unit.reshape(RIM, tile_cols, width)
        value_s[at : at + RIM, own_cols] = values.reshape(RIM, tile_cols, width)
    for side_ref, at in ((left_ref, 0), (right_ref, PAD + tile_cols)):
        unit, values = keyval(side_ref[...])
        shape = (2 * tile_rows, PAD, width)
        kept = slice(1, 1 + tile_rows + 2 * RIM)
        key_s[:, at : at + PAD] = unit.reshape(shape)[kept]
        value_s[:, at : at + PAD] = values.reshape(shape)[kept]

    key_rows = GROUP_ROWS + 2 * RIM
    key_cols = GROUP_COLS + 2 * PAD
    n_query = GROUP_ROWS * GROUP_COLS
    n_key = key_rows * key_cols
    col_groups = tile_cols // GROUP_COLS
    query_at = lax.broadcasted_iota(jnp.int32, (n_query, n_key), 0)
    key_at = lax.broadcasted_iota(jnp.int32, (n_query, n_key), 1)
    row_gap = key_at // key_cols - query_at // GROUP_COLS
    col_gap = key_at % key_cols - query_at % GROUP_COLS
    near = (
        (row_gap >= 0)
        & (row_gap <= 2 * RIM)
        & (col_gap >= PAD - RIM)
        & (col_gap <= PAD + RIM)
    )
    lane_head = lax.broadcasted_iota(jnp.int32, (1, QUAD), 1) // HEAD
    heads = QUAD // HEAD

    def attend_step(step, carry):
        row_at = (step // col_groups) * GROUP_ROWS
        col_at = pl.multiple_of((step % col_groups) * GROUP_COLS, GROUP_COLS)
        key_row = row_base + row_at - RIM + key_at // key_cols
        key_col = col_base + col_at - PAD + key_at % key_cols
        inside = (
            near & (key_row >= 0) & (key_row < image_rows) & (key_col >= 0) & (key_col < image_cols)
        )
        bias = jnp.where(inside, 0.0, -1e30)
        for start in range(0, width, QUAD):
            lanes = slice(start, start + QUAD)
            query = query_s[pl.ds(row_at, GROUP_ROWS), pl.ds(col_at, GROUP_COLS), lanes]
            query = query.reshape(n_query, QUAD)
            keys = key_s[pl.ds(row_at, key_rows), pl.ds(col_at, key_cols), lanes]
            keys = keys.reshape(n_key, QUAD)
            values = value_s[pl.ds(row_at, key_rows), pl.ds(col_at, key_cols), lanes]
            values = values.reshape(n_key, QUAD)
            spread = jnp.concatenate(
                [
                    query * (lane_head == h).astype(jnp.float32).astype(jnp.bfloat16)
                    for h in range(heads)
                ],
                axis=0,
            )
            scores = dot_nt(spread, keys)
            scores = (scores.reshape(heads, n_query, n_key) + bias[None]).reshape(-1, n_key)
            top = jnp.max(scores, axis=1, keepdims=True)
            expo = jnp.exp(scores - top)
            inverse = 1.0 / jnp.sum(expo, axis=1, keepdims=True)
            mixed = dot((expo * inverse).astype(jnp.bfloat16), values)
            joined = mixed[:n_query]
            for h in range(1, heads):
                part = mixed[h * n_query : (h + 1) * n_query]
                joined = jnp.where(lane_head == h, part, joined)
            attended_s[pl.ds(row_at, GROUP_ROWS), pl.ds(col_at, GROUP_COLS), lanes] = (
                joined.astype(jnp.bfloat16).reshape(GROUP_ROWS, GROUP_COLS, QUAD)
            )
        return carry

    lax.fori_loop(0, (tile_rows // GROUP_ROWS) * col_groups, attend_step, 0)

    def out_step(step, carry):
        rows = pl.ds(step * 2, 2)
        resid = image_ref[rows].astype(jnp.float32) + skip_ref[rows].astype(jnp.float32)
        projected = dot(attended_s[rows].reshape(2 * tile_cols, width), w_out_ref[...])
        out_ref[rows] = (resid + projected.reshape(2, tile_cols, width)).astype(jnp.bfloat16)
        return carry

    lax.fori_loop(0, tile_rows // 2, out_step, 0)


def attend(own, up, down, left, right, skip, image, w_qkv, w_out, scale):
    tile_rows, tile_cols, width = image.shape
    vmem = pl.BlockSpec(memory_space=pltpu.VMEM)
    extended = (tile_rows + 2 * RIM, tile_cols + 2 * PAD, width)
    return pl.pallas_call(
        attend_kernel,
        out_shape=jax.ShapeDtypeStruct(image.shape, jnp.bfloat16),
        in_specs=[vmem] * 10,
        out_specs=vmem,
        scratch_shapes=[
            pltpu.VMEM(image.shape, jnp.bfloat16),
            pltpu.VMEM(extended, jnp.bfloat16),
            pltpu.VMEM(extended, jnp.bfloat16),
            pltpu.VMEM(image.shape, jnp.bfloat16),
        ],
        compiler_params=pltpu.CompilerParams(vmem_limit_bytes=56 << 20),
        name="attend",
    )(own, up, down, left, right, skip, image, w_qkv, w_out, scale)


def local(image, skip_rows, owners, positions, gain, w_qkv, w_out, head_scale):
    own, skip, up, down, left, right = place(
        skip_rows, owners.reshape(1, -1), positions.reshape(1, -1), image, gain[None, :]
    )
    scale = jnp.repeat(head_scale, HEAD)[None, :]
    return attend(own, up, down, left, right, skip, image, w_qkv, w_out, scale)


def solution(mesh):
    in_specs = (
        P("row", "col", None),
        P(("row", "col"), None),
        P(("row", "col"), None),
        P(("row", "col")),
        P(),
        P(),
        P(),
        P(),
    )
    out_specs = P("row", "col", None)
    return jax.shard_map(local, mesh=mesh, in_specs=in_specs, out_specs=out_specs, check_vma=False)
```

```python
import functools

import jax
import jax.numpy as jnp
from jax import lax
from jax.experimental import pallas as pl
from jax.experimental.pallas import tpu as pltpu
from jax.sharding import PartitionSpec as P

RIM = 3
PAD = 4
CHUNKS = 4
GROUP_ROWS = 4
GROUP_COLS = 16
HEAD = 64
QUAD = 256
SLOTS = 16
STRIDE = 49
STRIDE_INVERSE = 81
MESH = pl.DeviceIdType.MESH


def dot(a, b):
    return jnp.dot(a, b, preferred_element_type=jnp.float32)


def dot_nt(a, b):
    return lax.dot_general(a, b, (((1,), (1,)), ((), ())), preferred_element_type=jnp.float32)


def head_sums(x, ones):
    square = x * x
    high = square.astype(jnp.bfloat16)
    low = (square - high.astype(jnp.float32)).astype(jnp.bfloat16)
    width = x.shape[1]
    parts = []
    for start in range(0, width, QUAD):
        lanes = slice(start, start + QUAD)
        parts.append(dot(high[:, lanes], ones) + dot(low[:, lanes], ones))
    return jnp.concatenate(parts, axis=1)


def flag(condition):
    return jnp.where(condition, 1.0, 0.0).astype(jnp.bfloat16)


def coordinates(row, col):
    return col // 2, (col % 2) * 2 + (row // 2) % 2, row // 4, row % 2


def level_kernel(
    rows_ref, owner_ref, position_ref, scale_ref, gain_ref, image_ref, w_qkv_ref, w_out_ref,
    out_ref,
    send_s, got_s, cell_send_s, cell_got_s, total_s, own_s, left_s, right_s,
    up_land, down_land, left_land, right_land,
    image_s, w_qkv_s, w_out_s, query_s, key_s, value_s, attended_s, score_s,
    send_sem, cell_send_sem, got_sems, cell_got_sems, halo_send_sems, halo_got_sems, load_sems,
):
    n_row, n_col = lax.axis_size("row"), lax.axis_size("col")
    n_device = n_row * n_col
    n_held, width = rows_ref.shape
    tile_rows, tile_cols, _ = image_ref.shape
    n_cell = tile_rows * tile_cols
    my_row, my_col = lax.axis_index("row"), lax.axis_index("col")
    my_x, my_y, my_z, my_core = coordinates(my_row, my_col)
    chunk = 16
    chunk_slots = chunk * SLOTS
    n_chunk = n_device // chunk

    def partner(step):
        gap = (step * STRIDE) % n_device
        x = (my_x + gap // 32) % 4
        y = (my_y + (gap // 8) % 4) % 4
        z = (my_z + (gap // 2) % 4) % 4
        core = (my_core + gap % 2) % 2
        return (z * 4 + (y % 2) * 2 + core, x * 2 + y // 2)

    loads = [
        pltpu.make_async_copy(src, dst, load_sems.at[index])
        for index, (src, dst) in enumerate(
            ((image_ref, image_s), (w_qkv_ref, w_qkv_s), (w_out_ref, w_out_s))
        )
    ]
    loads[0].start()
    up_land[...] = jnp.zeros_like(up_land)
    down_land[...] = jnp.zeros_like(down_land)
    left_land[...] = jnp.zeros_like(left_land)
    right_land[...] = jnp.zeros_like(right_land)

    barrier = pltpu.get_barrier_semaphore()

    def greet(step, carry):
        pl.semaphore_signal(barrier, inc=1, device_id=partner(step), device_id_type=MESH)
        return carry

    lax.fori_loop(1, n_device, greet, 0)

    owner = owner_ref[...]
    owner_row, owner_col = owner >> 3, owner & 7
    gap_x = ((owner_col >> 1) - my_x) & 3
    gap_y = ((owner_col & 1) * 2 + ((owner_row >> 1) & 1) - my_y) & 3
    gap_z = ((owner_row >> 2) - my_z) & 3
    gap_core = ((owner_row & 1) - my_core) & 1
    order = ((((gap_x * 4 + gap_y) * 4 + gap_z) * 2 + gap_core) * STRIDE_INVERSE) & (n_device - 1)
    holds = lax.broadcasted_iota(jnp.int32, (n_device, n_held), 0) == order
    holds_f = jnp.where(holds, 1.0, 0.0)
    holds_b = holds_f.astype(jnp.bfloat16)
    earlier = jnp.zeros((n_device, n_held), jnp.float32)
    for start in range(0, n_held, 256):
        at = lax.broadcasted_iota(jnp.int32, (256, n_held), 0) + start
        to = lax.broadcasted_iota(jnp.int32, (256, n_held), 1)
        earlier = earlier + dot(holds_b[:, start : start + 256], flag(at < to))
    rank = jnp.sum(earlier * holds_f, axis=0, keepdims=True).astype(jnp.int32)
    slot = order * SLOTS + rank
    code = position_ref[...] + 1
    lane = lax.broadcasted_iota(jnp.int32, (128, n_held), 0)
    parts = jnp.where(lane == rank, (code >> 5).astype(jnp.float32), 0.0)
    parts = parts + jnp.where(lane == rank + SLOTS, (code & 31).astype(jnp.float32), 0.0)
    cell_send_s[...] = dot_nt(holds_b, parts.astype(jnp.bfloat16))[:, None, :]


    def row_copy(step):
        return pltpu.make_async_remote_copy(
            src_ref=send_s.at[step],
            dst_ref=got_s.at[step],
            send_sem=send_sem,
            recv_sem=got_sems.at[step // chunk],
            device_id=partner(step),
            device_id_type=MESH,
        )

    def cell_copy(step):
        return pltpu.make_async_remote_copy(
            src_ref=cell_send_s.at[step],
            dst_ref=cell_got_s.at[step],
            send_sem=cell_send_sem,
            recv_sem=cell_got_sems.at[step // chunk],
            device_id=partner(step),
            device_id_type=MESH,
        )

    def pack(index):
        at = lax.broadcasted_iota(jnp.int32, (chunk_slots, n_held), 0) + index * chunk_slots
        packed = dot(flag(at == slot), rows_ref[...])
        send_s[pl.ds(index * chunk, chunk)] = packed.astype(jnp.bfloat16).reshape(
            chunk, SLOTS, width
        )

    def send(step, carry):
        cell_copy(step).start()
        row_copy(step).start()
        return carry

    pack(0)
    pl.semaphore_wait(barrier, n_device - 1)
    pltpu.make_async_copy(send_s.at[0], got_s.at[0], got_sems.at[0]).start()
    pltpu.make_async_copy(cell_send_s.at[0], cell_got_s.at[0], cell_got_sems.at[0]).start()
    lax.fori_loop(1, chunk, send, 0)

    def pack_step(index, carry):
        pack(index)
        lax.fori_loop(index * chunk, (index + 1) * chunk, send, 0)
        return carry

    lax.fori_loop(1, n_chunk, pack_step, 0)
    loads[0].wait()
    loads[1].start()
    loads[2].start()

    def fill_step(row, carry):
        rows = pl.ds(pl.multiple_of(row * tile_cols, tile_cols), tile_cols)
        total_s[rows] = image_s[row].astype(jnp.float32)
        return carry

    lax.fori_loop(0, tile_rows, fill_step, 0)

    table_at = lax.broadcasted_iota(jnp.int32, (128, chunk_slots), 0)
    table_slot = lax.broadcasted_iota(jnp.int32, (128, chunk_slots), 1) % SLOTS
    table = jnp.where(table_at == table_slot, 32.0, 0.0)
    table = table + jnp.where(table_at == table_slot + SLOTS, 1.0, 0.0)
    table = table.astype(jnp.bfloat16)
    source_at = lax.broadcasted_iota(jnp.int32, (chunk, chunk_slots), 0)
    source_slot = lax.broadcasted_iota(jnp.int32, (chunk, chunk_slots), 1) // SLOTS

    def unpack_step(index, carry):
        blocks = pl.ds(index * chunk, chunk)
        pltpu.make_async_copy(
            cell_got_s.at[blocks], cell_got_s.at[blocks], cell_got_sems.at[index]
        ).wait()
        codes = dot(cell_got_s[blocks].reshape(chunk, 128).astype(jnp.bfloat16), table)
        code_row = jnp.sum(
            jnp.where(source_at == source_slot, codes, 0.0), axis=0, keepdims=True
        ).astype(jnp.int32)
        cell = lax.broadcasted_iota(jnp.int32, (n_cell, chunk_slots), 0) + 1
        chosen = flag(cell == code_row)
        pltpu.make_async_copy(got_s.at[blocks], got_s.at[blocks], got_sems.at[index]).wait()
        total_s[...] += dot(chosen, got_s[blocks].reshape(chunk_slots, width))
        return carry

    lax.fori_loop(0, n_chunk, unpack_step, 0)

    def norm(start, count):
        resid = total_s[start * tile_cols : (start + count) * tile_cols]
        mean = jnp.mean(resid * resid, axis=-1, keepdims=True)
        normed = resid * lax.rsqrt(mean + 1e-06) * gain_ref[...]
        own_s[start : start + count] = normed.astype(jnp.bfloat16).reshape(
            count, tile_cols, width
        )

    def halo(index, there, src, dst):
        return pltpu.make_async_remote_copy(
            src_ref=src,
            dst_ref=dst,
            send_sem=halo_send_sems.at[index],
            recv_sem=halo_got_sems.at[index],
            device_id=there,
            device_id_type=MESH,
        )

    has_up, has_down = my_row > 0, my_row < n_row - 1
    has_left, has_right = my_col > 0, my_col < n_col - 1
    above, below = my_row - 1, my_row + 1
    before, after = my_col - 1, my_col + 1
    side = tile_rows * PAD
    half = side // 2
    top, bottom = pl.ds(0, half), pl.ds(half, half)
    near_top, middle, near_bottom = pl.ds(0, half), pl.ds(half, side), pl.ds(half + side, half)
    moves = []
    chunk_cols = tile_cols // CHUNKS
    for sends, gets, there, at, land in (
        (has_up, has_down, (above, my_col), 0, down_land),
        (has_down, has_up, (below, my_col), tile_rows - RIM, up_land),
    ):
        for index in range(CHUNKS):
            cols = pl.ds(index * chunk_cols, chunk_cols)
            moves.append((sends, gets, there, own_s.at[pl.ds(at, RIM), cols], land.at[index]))
    moves += [
        (has_left, has_right, (my_row, before), left_s, right_land.at[middle]),
        (has_right, has_left, (my_row, after), right_s, left_land.at[middle]),
        (
            has_up & has_left, has_down & has_right, (above, before),
            left_s.at[top], right_land.at[near_bottom],
        ),
        (
            has_up & has_right, has_down & has_left, (above, after),
            right_s.at[top], left_land.at[near_bottom],
        ),
        (
            has_down & has_left, has_up & has_right, (below, before),
            left_s.at[bottom], right_land.at[near_top],
        ),
        (
            has_down & has_right, has_up & has_left, (below, after),
            right_s.at[bottom], left_land.at[near_top],
        ),
    ]

    def start_move(index):
        sends, _, there, src, dst = moves[index]

        @pl.when(sends)
        def _():
            halo(index, there, src, dst).start()

    def end_move(index):
        _, gets, there, src, dst = moves[index]

        @pl.when(gets)
        def _():
            halo(index, there, src, dst).wait_recv()

    norm(0, RIM)
    start_move(0)
    start_move(1)
    norm(tile_rows - RIM, RIM)
    start_move(CHUNKS)
    start_move(CHUNKS + 1)
    norm(RIM, tile_rows - 2 * RIM)
    edge = 16
    pick_at = lax.broadcasted_iota(jnp.int32, (side, tile_rows * edge), 0)
    pick_from = lax.broadcasted_iota(jnp.int32, (side, tile_rows * edge), 1)
    pick_row, pick_col = pick_at // PAD, pick_at % PAD
    pick = flag((pick_from // edge == pick_row) & (pick_from % edge == pick_col))
    first = dot(pick, own_s[:, :edge].reshape(tile_rows * edge, width))
    left_s[...] = first.astype(jnp.bfloat16)
    pick_col = pick_col + edge - PAD
    pick = flag((pick_from // edge == pick_row) & (pick_from % edge == pick_col))
    last = dot(pick, own_s[:, tile_cols - edge :].reshape(tile_rows * edge, width))
    right_s[...] = last.astype(jnp.bfloat16)
    for index in range(2 * CHUNKS, len(moves)):
        start_move(index)
    for index in range(2, CHUNKS):
        start_move(index)
        start_move(CHUNKS + index)

    loads[1].wait()
    lane_a = lax.broadcasted_iota(jnp.int32, (QUAD, QUAD), 0) // HEAD
    lane_b = lax.broadcasted_iota(jnp.int32, (QUAD, QUAD), 1) // HEAD
    ones = flag(lane_a == lane_b)
    head_at = lax.broadcasted_iota(jnp.int32, (1, width), 1) // HEAD
    scale = jnp.zeros((1, width), jnp.float32)
    for head in range(width // HEAD):
        scale = jnp.where(head_at == head, scale_ref[head], scale)

    def keyval(x):
        keys = dot(x, w_qkv_s[:, width : 2 * width]).astype(jnp.bfloat16)
        keys = keys.astype(jnp.float32)
        unit = keys * lax.rsqrt(head_sums(keys, ones) + 1e-06)
        values = dot(x, w_qkv_s[:, 2 * width :])
        return unit, values

    own_cols = slice(PAD, PAD + tile_cols)

    def own_step(step, carry):
        shape = (2, tile_cols, width)
        x = own_s[pl.ds(step * 2, 2)].reshape(2 * tile_cols, width)
        unit, values = keyval(x)
        key_s[pl.ds(step * 2 + RIM, 2), own_cols] = unit.reshape(shape)
        value_s[pl.ds(step * 2 + RIM, 2), own_cols] = values.reshape(shape)
        queries = dot(x, w_qkv_s[:, :width])
        unit = queries * scale * lax.rsqrt(head_sums(queries, ones) + 1e-06)
        query_s[pl.ds(step * 2, 2)] = unit.astype(jnp.bfloat16).reshape(shape)
        return carry

    lax.fori_loop(0, tile_rows // 2, own_step, 0)

    def rim_step(index):
        end_move(index)
        end_move(CHUNKS + index)
        n_rim = RIM * chunk_cols
        x = jnp.concatenate(
            [up_land[index].reshape(n_rim, width), down_land[index].reshape(n_rim, width)], axis=0
        )
        unit, values = keyval(x)
        shape = (RIM, chunk_cols, width)
        cols = slice(PAD + index * chunk_cols, PAD + (index + 1) * chunk_cols)
        for at, part in ((0, slice(0, n_rim)), (RIM + tile_rows, slice(n_rim, 2 * n_rim))):
            key_s[at : at + RIM, cols] = unit[part].reshape(shape)
            value_s[at : at + RIM, cols] = values[part].reshape(shape)

    def side_step():
        for index in range(2 * CHUNKS, len(moves)):
            end_move(index)
        n_side = 2 * side
        at = lax.broadcasted_iota(jnp.int32, (2 * n_side, 2 * n_side), 0)
        source = lax.broadcasted_iota(jnp.int32, (2 * n_side, 2 * n_side), 1)
        spot = at % (2 * PAD)
        wanted = (spot // PAD) * n_side + (at // (2 * PAD)) * PAD + spot % PAD
        x = jnp.concatenate([left_land[...], right_land[...]], axis=0)
        x = dot(flag(source == wanted), x).astype(jnp.bfloat16)
        unit, values = keyval(x)
        n_ext = tile_rows + 2 * RIM
        is_left = lax.broadcasted_iota(jnp.int32, (n_ext, 2 * PAD, width), 1) < PAD
        left_cols, right_cols = slice(0, 2 * PAD), slice(tile_cols, tile_cols + 2 * PAD)
        for ref, new in ((key_s, unit), (value_s, values)):
            new = new.reshape(2 * tile_rows, 2 * PAD, width)[1 : 1 + n_ext]
            ref[:, left_cols] = jnp.where(is_left, new, ref[:, left_cols])
            ref[:, right_cols] = jnp.where(is_left, ref[:, right_cols], new)

    image_rows, image_cols = tile_rows * n_row, tile_cols * n_col
    row_base, col_base = my_row * tile_rows, my_col * tile_cols
    key_rows = GROUP_ROWS + 2 * RIM
    key_cols = GROUP_COLS + 2 * PAD
    n_query = GROUP_ROWS * GROUP_COLS
    n_key = key_rows * key_cols
    col_groups = tile_cols // GROUP_COLS
    query_at = lax.broadcasted_iota(jnp.int32, (n_query, n_key), 0)
    key_at = lax.broadcasted_iota(jnp.int32, (n_query, n_key), 1)
    key_row_at, key_col_at = key_at // key_cols, key_at % key_cols
    row_gap = key_row_at - query_at // GROUP_COLS
    col_gap = key_col_at - query_at % GROUP_COLS
    near = (
        (row_gap >= 0)
        & (row_gap <= 2 * RIM)
        & (col_gap >= PAD - RIM)
        & (col_gap <= PAD + RIM)
    )
    lane_head = lax.broadcasted_iota(jnp.int32, (1, QUAD), 1) // HEAD
    heads = QUAD // HEAD
    masks = [flag(lane_head == head) for head in range(heads)]
    quads = range(0, width, QUAD)

    def window(ref, band, col_at, lanes):
        rows = slice(band * GROUP_ROWS, band * GROUP_ROWS + key_rows)
        block = ref[rows, pl.ds(col_at, key_cols), lanes]
        return block.reshape(n_key, QUAD).astype(jnp.bfloat16)

    def score(band, group):
        col_at = pl.multiple_of(group * GROUP_COLS, GROUP_COLS)
        rows = slice(band * GROUP_ROWS, (band + 1) * GROUP_ROWS)
        for index, start in enumerate(quads):
            lanes = slice(start, start + QUAD)
            query = query_s[rows, pl.ds(col_at, GROUP_COLS), lanes].reshape(n_query, QUAD)
            spread = jnp.concatenate([query * mask for mask in masks], axis=0)
            score_s[band, index] = dot_nt(spread, window(key_s, band, col_at, lanes))

    def mix(band, group):
        col_at = pl.multiple_of(group * GROUP_COLS, GROUP_COLS)
        rows = slice(band * GROUP_ROWS, (band + 1) * GROUP_ROWS)
        key_row = row_base + band * GROUP_ROWS - RIM + key_row_at
        key_col = col_base + col_at - PAD + key_col_at
        inside = (
            near & (key_row >= 0) & (key_row < image_rows) & (key_col >= 0) & (key_col < image_cols)
        )
        bias = jnp.where(inside, 0.0, -1e30)
        for index, start in enumerate(quads):
            lanes = slice(start, start + QUAD)
            scores = score_s[band, index].reshape(heads, n_query, n_key) + bias[None]
            scores = scores.reshape(heads * n_query, n_key)
            top = jnp.max(scores, axis=1, keepdims=True)
            expo = jnp.exp(scores - top)
            inverse = 1.0 / jnp.sum(expo, axis=1, keepdims=True)
            weights = (expo * inverse).astype(jnp.bfloat16)
            mixed = dot(weights, window(value_s, band, col_at, lanes))
            joined = mixed[:n_query]
            for h in range(1, heads):
                part = mixed[h * n_query : (h + 1) * n_query]
                joined = jnp.where(lane_head == h, part, joined)
            attended_s[rows, pl.ds(col_at, GROUP_COLS), lanes] = joined.astype(
                jnp.bfloat16
            ).reshape(GROUP_ROWS, GROUP_COLS, QUAD)

    bands = tile_rows // GROUP_ROWS

    def attend(first, end):
        score(0, first)

        def step(group, carry):
            for band in range(bands):
                if band + 1 < bands:
                    score(band + 1, group)
                else:
                    score(0, jnp.minimum(group + 1, col_groups - 1))
                mix(band, group)
            return carry

        lax.fori_loop(first, end, step, 0)

    rim_step(0)
    rim_step(1)
    side_step()
    attend(0, 3)
    rim_step(2)
    attend(3, 5)
    rim_step(3)
    attend(5, col_groups)

    loads[2].wait()

    def out_step(step, carry):
        rows = pl.ds(step * 2, 2)
        flat = pl.ds(pl.multiple_of(step * 2 * tile_cols, 2 * tile_cols), 2 * tile_cols)
        projected = dot(attended_s[rows].reshape(2 * tile_cols, width), w_out_s[...])
        level = (total_s[flat] + projected).astype(jnp.bfloat16)
        out_ref[rows] = level.reshape(2, tile_cols, width)
        return carry

    lax.fori_loop(0, tile_rows // 2, out_step, 0)

    for index, (sends, _, there, src, dst) in enumerate(moves):

        @pl.when(sends)
        def _():
            halo(index, there, src, dst).wait_send()

    others = pl.ds(1, n_device - 1)
    pltpu.make_async_copy(send_s.at[others], got_s.at[others], send_sem).wait()
    pltpu.make_async_copy(cell_send_s.at[others], cell_got_s.at[others], cell_send_sem).wait()


def local(image, skip_rows, owners, positions, gain, w_qkv, w_out, head_scale):
    tile_rows, tile_cols, width = image.shape
    n_device = lax.axis_size("row") * lax.axis_size("col")
    vmem = pl.BlockSpec(memory_space=pltpu.VMEM)
    smem = pl.BlockSpec(memory_space=pltpu.SMEM)
    far = pl.BlockSpec(memory_space=pl.ANY)
    rim = (CHUNKS, RIM, tile_cols // CHUNKS, width)
    side = (tile_rows * PAD, width)
    sides = (2 * tile_rows * PAD, width)
    extended = (tile_rows + 2 * RIM, tile_cols + 4 * PAD, width)
    n_query = GROUP_ROWS * GROUP_COLS * QUAD // HEAD
    n_key = (GROUP_ROWS + 2 * RIM) * (GROUP_COLS + 2 * PAD)
    bf16, f32 = jnp.bfloat16, jnp.float32
    n_chunk = n_device // 16
    n_move = 2 * CHUNKS + 6
    return pl.pallas_call(
        level_kernel,
        out_shape=jax.ShapeDtypeStruct(image.shape, bf16),
        in_specs=[vmem, vmem, vmem, smem, vmem, far, far, far],
        out_specs=vmem,
        scratch_shapes=[
            pltpu.VMEM((n_device, SLOTS, width), bf16),
            pltpu.VMEM((n_device, SLOTS, width), bf16),
            pltpu.VMEM((n_device, 1, 128), f32),
            pltpu.VMEM((n_device, 1, 128), f32),
            pltpu.VMEM((tile_rows * tile_cols, width), f32),
            pltpu.VMEM(image.shape, bf16),
            pltpu.VMEM(side, bf16),
            pltpu.VMEM(side, bf16),
            pltpu.VMEM(rim, bf16),
            pltpu.VMEM(rim, bf16),
            pltpu.VMEM(sides, bf16),
            pltpu.VMEM(sides, bf16),
            pltpu.VMEM(image.shape, bf16),
            pltpu.VMEM(w_qkv.shape, bf16),
            pltpu.VMEM(w_out.shape, bf16),
            pltpu.VMEM(image.shape, bf16),
            pltpu.VMEM(extended, f32),
            pltpu.VMEM(extended, f32),
            pltpu.VMEM(image.shape, bf16),
            pltpu.VMEM((tile_rows // GROUP_ROWS, width // QUAD, n_query, n_key), f32),
            pltpu.SemaphoreType.DMA,
            pltpu.SemaphoreType.DMA,
            pltpu.SemaphoreType.DMA((n_chunk,)),
            pltpu.SemaphoreType.DMA((n_chunk,)),
            pltpu.SemaphoreType.DMA((n_move,)),
            pltpu.SemaphoreType.DMA((n_move,)),
            pltpu.SemaphoreType.DMA((3,)),
        ],
        compiler_params=pltpu.CompilerParams(
            collective_id=0, has_side_effects=True, vmem_limit_bytes=60 << 20
        ),
        name="level",
    )(
        skip_rows,
        owners.reshape(1, -1),
        positions.reshape(1, -1),
        head_scale,
        gain,
        image,
        w_qkv,
        w_out,
    )


def solution(mesh):
    in_specs = (
        P("row", "col", None),
        P(("row", "col"), None),
        P(("row", "col"), None),
        P(("row", "col")),
        P(),
        P(),
        P(),
        P(),
    )
    out_specs = P("row", "col", None)
    return jax.shard_map(local, mesh=mesh, in_specs=in_specs, out_specs=out_specs, check_vma=False)
```

```python
import functools

import jax
import jax.numpy as jnp
from jax import lax
from jax.experimental import pallas as pl
from jax.experimental.pallas import tpu as pltpu
from jax.sharding import PartitionSpec as P

RIM = 3
PAD = 4
CHUNKS = 4
GROUP_ROWS = 4
GROUP_COLS = 16
HEAD = 64
QUAD = 256
SLOTS = 16
STRIDE = 49
STRIDE_INVERSE = 81
MESH = pl.DeviceIdType.MESH


def dot(a, b):
    return jnp.dot(a, b, preferred_element_type=jnp.float32)


def dot_nt(a, b):
    return lax.dot_general(a, b, (((1,), (1,)), ((), ())), preferred_element_type=jnp.float32)


def head_sums(x, ones):
    square = x * x
    high = square.astype(jnp.bfloat16)
    low = (square - high.astype(jnp.float32)).astype(jnp.bfloat16)
    width = x.shape[1]
    parts = []
    for start in range(0, width, QUAD):
        lanes = slice(start, start + QUAD)
        parts.append(dot(high[:, lanes], ones) + dot(low[:, lanes], ones))
    return jnp.concatenate(parts, axis=1)


def flag(condition):
    return jnp.where(condition, 1.0, 0.0).astype(jnp.bfloat16)


def coordinates(row, col):
    return col // 2, (col % 2) * 2 + (row // 2) % 2, row // 4, row % 2


def level_kernel(
    rows_ref, owner_ref, position_ref, scale_ref, gain_ref, image_ref, w_qkv_ref, w_out_ref,
    out_ref,
    send_s, got_s, cell_send_s, cell_got_s, total_s, own_s, left_s, right_s,
    up_land, down_land, left_land, right_land,
    image_s, w_qkv_s, w_out_s, query_s, key_s, value_s, attended_s, score_s,
    send_sem, cell_send_sem, got_sems, cell_got_sems, halo_send_sems, halo_got_sems, load_sems, meet_sems,
):
    n_row, n_col = lax.axis_size("row"), lax.axis_size("col")
    n_device = n_row * n_col
    n_held, width = rows_ref.shape
    tile_rows, tile_cols, _ = image_ref.shape
    n_cell = tile_rows * tile_cols
    my_row, my_col = lax.axis_index("row"), lax.axis_index("col")
    my_x, my_y, my_z, my_core = coordinates(my_row, my_col)
    chunk = 16
    chunk_slots = chunk * SLOTS
    n_chunk = n_device // chunk

    def shifted(x_gap, y_gap, z_gap, core_gap):
        x, y, z = (my_x + x_gap) % 4, (my_y + y_gap) % 4, (my_z + z_gap) % 4
        core = (my_core + core_gap) % 2
        return (z * 4 + (y % 2) * 2 + core, x * 2 + y // 2)

    def partner(step):
        gap = (step * STRIDE) % n_device
        return shifted(gap // 32, (gap // 8) % 4, (gap // 2) % 4, gap % 2)

    x_peers = [(gap, 0, 0, 0) for gap in range(1, 4)]
    y_peers = [(0, gap, 0, 0) for gap in range(1, 4)]
    z_peers = [(0, 0, gap // 2, gap % 2) for gap in range(1, 8)]

    def signal(semaphore, peers):
        for peer in peers:
            pl.semaphore_signal(
                semaphore, inc=1, device_id=shifted(*peer), device_id_type=MESH
            )

    up_land[...] = jnp.zeros_like(up_land)
    down_land[...] = jnp.zeros_like(down_land)
    left_land[...] = jnp.zeros_like(left_land)
    right_land[...] = jnp.zeros_like(right_land)
    barrier = pltpu.get_barrier_semaphore()
    signal(barrier, x_peers + y_peers + z_peers)

    loads = [
        pltpu.make_async_copy(src, dst, load_sems.at[index])
        for index, (src, dst) in enumerate(
            ((image_ref, image_s), (w_qkv_ref, w_qkv_s), (w_out_ref, w_out_s))
        )
    ]
    loads[0].start()

    owner = owner_ref[...]
    owner_row, owner_col = owner >> 3, owner & 7
    gap_x = ((owner_col >> 1) - my_x) & 3
    gap_y = ((owner_col & 1) * 2 + ((owner_row >> 1) & 1) - my_y) & 3
    gap_z = ((owner_row >> 2) - my_z) & 3
    gap_core = ((owner_row & 1) - my_core) & 1
    order = ((((gap_x * 4 + gap_y) * 4 + gap_z) * 2 + gap_core) * STRIDE_INVERSE) & (n_device - 1)
    holds = lax.broadcasted_iota(jnp.int32, (n_device, n_held), 0) == order
    holds_f = jnp.where(holds, 1.0, 0.0)
    holds_b = holds_f.astype(jnp.bfloat16)
    earlier = jnp.zeros((n_device, n_held), jnp.float32)
    for start in range(0, n_held, 256):
        at = lax.broadcasted_iota(jnp.int32, (256, n_held), 0) + start
        to = lax.broadcasted_iota(jnp.int32, (256, n_held), 1)
        earlier = earlier + dot(holds_b[:, start : start + 256], flag(at < to))
    pl.semaphore_wait(barrier, len(x_peers + y_peers + z_peers))
    signal(meet_sems.at[0], y_peers)
    rank = jnp.sum(earlier * holds_f, axis=0, keepdims=True).astype(jnp.int32)
    slot = order * SLOTS + rank
    code = position_ref[...] + 1
    lane = lax.broadcasted_iota(jnp.int32, (128, n_held), 0)
    parts = jnp.where(lane == rank, (code >> 5).astype(jnp.float32), 0.0)
    parts = parts + jnp.where(lane == rank + SLOTS, (code & 31).astype(jnp.float32), 0.0)
    cell_send_s[...] = dot_nt(holds_b, parts.astype(jnp.bfloat16))[:, None, :]


    def row_copy(step):
        return pltpu.make_async_remote_copy(
            src_ref=send_s.at[step],
            dst_ref=got_s.at[step],
            send_sem=send_sem,
            recv_sem=got_sems.at[step // chunk],
            device_id=partner(step),
            device_id_type=MESH,
        )

    def cell_copy(step):
        return pltpu.make_async_remote_copy(
            src_ref=cell_send_s.at[step],
            dst_ref=cell_got_s.at[step],
            send_sem=cell_send_sem,
            recv_sem=cell_got_sems.at[step // chunk],
            device_id=partner(step),
            device_id_type=MESH,
        )

    def pack(index):
        at = lax.broadcasted_iota(jnp.int32, (chunk_slots, n_held), 0) + index * chunk_slots
        packed = dot(flag(at == slot), rows_ref[...])
        send_s[pl.ds(index * chunk, chunk)] = packed.astype(jnp.bfloat16).reshape(
            chunk, SLOTS, width
        )

    def send(step, carry):
        cell_copy(step).start()
        row_copy(step).start()
        return carry

    pl.semaphore_wait(meet_sems.at[0], len(y_peers))
    signal(meet_sems.at[1], z_peers)
    pack(0)
    pl.semaphore_wait(meet_sems.at[1], len(z_peers))
    pltpu.make_async_copy(send_s.at[0], got_s.at[0], got_sems.at[0]).start()
    pltpu.make_async_copy(cell_send_s.at[0], cell_got_s.at[0], cell_got_sems.at[0]).start()
    lax.fori_loop(1, chunk, send, 0)

    def pack_step(index, carry):
        pack(index)
        lax.fori_loop(index * chunk, (index + 1) * chunk, send, 0)
        return carry

    lax.fori_loop(1, n_chunk, pack_step, 0)
    loads[0].wait()
    loads[1].start()
    loads[2].start()

    def fill_step(row, carry):
        rows = pl.ds(pl.multiple_of(row * tile_cols, tile_cols), tile_cols)
        total_s[rows] = image_s[row].astype(jnp.float32)
        return carry

    lax.fori_loop(0, tile_rows, fill_step, 0)

    table_at = lax.broadcasted_iota(jnp.int32, (128, chunk_slots), 0)
    table_slot = lax.broadcasted_iota(jnp.int32, (128, chunk_slots), 1) % SLOTS
    table = jnp.where(table_at == table_slot, 32.0, 0.0)
    table = table + jnp.where(table_at == table_slot + SLOTS, 1.0, 0.0)
    table = table.astype(jnp.bfloat16)
    source_at = lax.broadcasted_iota(jnp.int32, (chunk, chunk_slots), 0)
    source_slot = lax.broadcasted_iota(jnp.int32, (chunk, chunk_slots), 1) // SLOTS

    def unpack_step(index, carry):
        blocks = pl.ds(index * chunk, chunk)
        pltpu.make_async_copy(
            cell_got_s.at[blocks], cell_got_s.at[blocks], cell_got_sems.at[index]
        ).wait()
        codes = dot(cell_got_s[blocks].reshape(chunk, 128).astype(jnp.bfloat16), table)
        code_row = jnp.sum(
            jnp.where(source_at == source_slot, codes, 0.0), axis=0, keepdims=True
        ).astype(jnp.int32)
        cell = lax.broadcasted_iota(jnp.int32, (n_cell, chunk_slots), 0) + 1
        chosen = flag(cell == code_row)
        pltpu.make_async_copy(got_s.at[blocks], got_s.at[blocks], got_sems.at[index]).wait()
        total_s[...] += dot(chosen, got_s[blocks].reshape(chunk_slots, width))
        return carry

    lax.fori_loop(0, n_chunk, unpack_step, 0)

    def norm(start, count):
        resid = total_s[start * tile_cols : (start + count) * tile_cols]
        mean = jnp.mean(resid * resid, axis=-1, keepdims=True)
        normed = resid * lax.rsqrt(mean + 1e-06) * gain_ref[...]
        own_s[start : start + count] = normed.astype(jnp.bfloat16).reshape(
            count, tile_cols, width
        )

    def halo(index, there, src, dst):
        return pltpu.make_async_remote_copy(
            src_ref=src,
            dst_ref=dst,
            send_sem=halo_send_sems.at[index],
            recv_sem=halo_got_sems.at[index],
            device_id=there,
            device_id_type=MESH,
        )

    has_up, has_down = my_row > 0, my_row < n_row - 1
    has_left, has_right = my_col > 0, my_col < n_col - 1
    above, below = my_row - 1, my_row + 1
    before, after = my_col - 1, my_col + 1
    side = tile_rows * PAD
    half = side // 2
    top, bottom = pl.ds(0, half), pl.ds(half, half)
    near_top, middle, near_bottom = pl.ds(0, half), pl.ds(half, side), pl.ds(half + side, half)
    moves = []
    chunk_cols = tile_cols // CHUNKS
    for sends, gets, there, at, land in (
        (has_up, has_down, (above, my_col), 0, down_land),
        (has_down, has_up, (below, my_col), tile_rows - RIM, up_land),
    ):
        for index in range(CHUNKS):
            cols = pl.ds(index * chunk_cols, chunk_cols)
            moves.append((sends, gets, there, own_s.at[pl.ds(at, RIM), cols], land.at[index]))
    moves += [
        (has_left, has_right, (my_row, before), left_s, right_land.at[middle]),
        (has_right, has_left, (my_row, after), right_s, left_land.at[middle]),
        (
            has_up & has_left, has_down & has_right, (above, before),
            left_s.at[top], right_land.at[near_bottom],
        ),
        (
            has_up & has_right, has_down & has_left, (above, after),
            right_s.at[top], left_land.at[near_bottom],
        ),
        (
            has_down & has_left, has_up & has_right, (below, before),
            left_s.at[bottom], right_land.at[near_top],
        ),
        (
            has_down & has_right, has_up & has_left, (below, after),
            right_s.at[bottom], left_land.at[near_top],
        ),
    ]

    def start_move(index):
        sends, _, there, src, dst = moves[index]

        @pl.when(sends)
        def _():
            halo(index, there, src, dst).start()

    def end_move(index):
        _, gets, there, src, dst = moves[index]

        @pl.when(gets)
        def _():
            halo(index, there, src, dst).wait_recv()

    norm(0, RIM)
    start_move(0)
    start_move(1)
    norm(tile_rows - RIM, RIM)
    start_move(CHUNKS)
    start_move(CHUNKS + 1)
    norm(RIM, tile_rows - 2 * RIM)
    edge = 16
    pick_at = lax.broadcasted_iota(jnp.int32, (side, tile_rows * edge), 0)
    pick_from = lax.broadcasted_iota(jnp.int32, (side, tile_rows * edge), 1)
    pick_row, pick_col = pick_at // PAD, pick_at % PAD
    pick = flag((pick_from // edge == pick_row) & (pick_from % edge == pick_col))
    first = dot(pick, own_s[:, :edge].reshape(tile_rows * edge, width))
    left_s[...] = first.astype(jnp.bfloat16)
    pick_col = pick_col + edge - PAD
    pick = flag((pick_from // edge == pick_row) & (pick_from % edge == pick_col))
    last = dot(pick, own_s[:, tile_cols - edge :].reshape(tile_rows * edge, width))
    right_s[...] = last.astype(jnp.bfloat16)
    for index in range(2 * CHUNKS, len(moves)):
        start_move(index)
    for index in range(2, CHUNKS):
        start_move(index)
        start_move(CHUNKS + index)

    loads[1].wait()
    lane_a = lax.broadcasted_iota(jnp.int32, (QUAD, QUAD), 0) // HEAD
    lane_b = lax.broadcasted_iota(jnp.int32, (QUAD, QUAD), 1) // HEAD
    ones = flag(lane_a == lane_b)
    head_at = lax.broadcasted_iota(jnp.int32, (1, width), 1) // HEAD
    scale = jnp.zeros((1, width), jnp.float32)
    for head in range(width // HEAD):
        scale = jnp.where(head_at == head, scale_ref[head], scale)

    def keyval(x):
        keys = dot(x, w_qkv_s[:, width : 2 * width]).astype(jnp.bfloat16)
        keys = keys.astype(jnp.float32)
        unit = keys * lax.rsqrt(head_sums(keys, ones) + 1e-06)
        values = dot(x, w_qkv_s[:, 2 * width :])
        return unit, values

    own_cols = slice(PAD, PAD + tile_cols)

    def own_step(step, carry):
        shape = (2, tile_cols, width)
        x = own_s[pl.ds(step * 2, 2)].reshape(2 * tile_cols, width)
        unit, values = keyval(x)
        key_s[pl.ds(step * 2 + RIM, 2), own_cols] = unit.reshape(shape)
        value_s[pl.ds(step * 2 + RIM, 2), own_cols] = values.reshape(shape)
        queries = dot(x, w_qkv_s[:, :width])
        unit = queries * scale * lax.rsqrt(head_sums(queries, ones) + 1e-06)
        query_s[pl.ds(step * 2, 2)] = unit.astype(jnp.bfloat16).reshape(shape)
        return carry

    lax.fori_loop(0, tile_rows // 2, own_step, 0)

    def rim_step(index):
        end_move(index)
        end_move(CHUNKS + index)
        n_rim = RIM * chunk_cols
        x = jnp.concatenate(
            [up_land[index].reshape(n_rim, width), down_land[index].reshape(n_rim, width)], axis=0
        )
        unit, values = keyval(x)
        shape = (RIM, chunk_cols, width)
        cols = slice(PAD + index * chunk_cols, PAD + (index + 1) * chunk_cols)
        for at, part in ((0, slice(0, n_rim)), (RIM + tile_rows, slice(n_rim, 2 * n_rim))):
            key_s[at : at + RIM, cols] = unit[part].reshape(shape)
            value_s[at : at + RIM, cols] = values[part].reshape(shape)

    def side_step():
        for index in range(2 * CHUNKS, len(moves)):
            end_move(index)
        n_side = 2 * side
        at = lax.broadcasted_iota(jnp.int32, (2 * n_side, 2 * n_side), 0)
        source = lax.broadcasted_iota(jnp.int32, (2 * n_side, 2 * n_side), 1)
        spot = at % (2 * PAD)
        wanted = (spot // PAD) * n_side + (at // (2 * PAD)) * PAD + spot % PAD
        x = jnp.concatenate([left_land[...], right_land[...]], axis=0)
        x = dot(flag(source == wanted), x).astype(jnp.bfloat16)
        unit, values = keyval(x)
        n_ext = tile_rows + 2 * RIM
        is_left = lax.broadcasted_iota(jnp.int32, (n_ext, 2 * PAD, width), 1) < PAD
        left_cols, right_cols = slice(0, 2 * PAD), slice(tile_cols, tile_cols + 2 * PAD)
        for ref, new in ((key_s, unit), (value_s, values)):
            new = new.reshape(2 * tile_rows, 2 * PAD, width)[1 : 1 + n_ext]
            ref[:, left_cols] = jnp.where(is_left, new, ref[:, left_cols])
            ref[:, right_cols] = jnp.where(is_left, ref[:, right_cols], new)

    image_rows, image_cols = tile_rows * n_row, tile_cols * n_col
    row_base, col_base = my_row * tile_rows, my_col * tile_cols
    key_rows = GROUP_ROWS + 2 * RIM
    key_cols = GROUP_COLS + 2 * PAD
    n_query = GROUP_ROWS * GROUP_COLS
    n_key = key_rows * key_cols
    col_groups = tile_cols // GROUP_COLS
    query_at = lax.broadcasted_iota(jnp.int32, (n_query, n_key), 0)
    key_at = lax.broadcasted_iota(jnp.int32, (n_query, n_key), 1)
    key_row_at, key_col_at = key_at // key_cols, key_at % key_cols
    row_gap = key_row_at - query_at // GROUP_COLS
    col_gap = key_col_at - query_at % GROUP_COLS
    near = (
        (row_gap >= 0)
        & (row_gap <= 2 * RIM)
        & (col_gap >= PAD - RIM)
        & (col_gap <= PAD + RIM)
    )
    lane_head = lax.broadcasted_iota(jnp.int32, (1, QUAD), 1) // HEAD
    heads = QUAD // HEAD
    masks = [flag(lane_head == head) for head in range(heads)]
    quads = range(0, width, QUAD)

    def window(ref, band, col_at, lanes):
        rows = slice(band * GROUP_ROWS, band * GROUP_ROWS + key_rows)
        block = ref[rows, pl.ds(col_at, key_cols), lanes]
        return block.reshape(n_key, QUAD).astype(jnp.bfloat16)

    def score(band, group):
        col_at = pl.multiple_of(group * GROUP_COLS, GROUP_COLS)
        rows = slice(band * GROUP_ROWS, (band + 1) * GROUP_ROWS)
        for index, start in enumerate(quads):
            lanes = slice(start, start + QUAD)
            query = query_s[rows, pl.ds(col_at, GROUP_COLS), lanes].reshape(n_query, QUAD)
            spread = jnp.concatenate([query * mask for mask in masks], axis=0)
            score_s[band, index] = dot_nt(spread, window(key_s, band, col_at, lanes))

    def mix(band, group):
        col_at = pl.multiple_of(group * GROUP_COLS, GROUP_COLS)
        rows = slice(band * GROUP_ROWS, (band + 1) * GROUP_ROWS)
        key_row = row_base + band * GROUP_ROWS - RIM + key_row_at
        key_col = col_base + col_at - PAD + key_col_at
        inside = (
            near & (key_row >= 0) & (key_row < image_rows) & (key_col >= 0) & (key_col < image_cols)
        )
        bias = jnp.where(inside, 0.0, -1e30)
        for index, start in enumerate(quads):
            lanes = slice(start, start + QUAD)
            scores = score_s[band, index].reshape(heads, n_query, n_key) + bias[None]
            scores = scores.reshape(heads * n_query, n_key)
            top = jnp.max(scores, axis=1, keepdims=True)
            expo = jnp.exp(scores - top)
            inverse = 1.0 / jnp.sum(expo, axis=1, keepdims=True)
            weights = (expo * inverse).astype(jnp.bfloat16)
            mixed = dot(weights, window(value_s, band, col_at, lanes))
            joined = mixed[:n_query]
            for h in range(1, heads):
                part = mixed[h * n_query : (h + 1) * n_query]
                joined = jnp.where(lane_head == h, part, joined)
            attended_s[rows, pl.ds(col_at, GROUP_COLS), lanes] = joined.astype(
                jnp.bfloat16
            ).reshape(GROUP_ROWS, GROUP_COLS, QUAD)

    bands = tile_rows // GROUP_ROWS

    def attend(first, end):
        score(0, first)

        def step(group, carry):
            for band in range(bands):
                if band + 1 < bands:
                    score(band + 1, group)
                else:
                    score(0, jnp.minimum(group + 1, col_groups - 1))
                mix(band, group)
            return carry

        lax.fori_loop(first, end, step, 0)

    rim_step(0)
    rim_step(1)
    side_step()
    attend(0, 3)
    rim_step(2)
    attend(3, 5)
    rim_step(3)
    attend(5, col_groups)

    loads[2].wait()

    def out_step(step, carry):
        rows = pl.ds(step * 2, 2)
        flat = pl.ds(pl.multiple_of(step * 2 * tile_cols, 2 * tile_cols), 2 * tile_cols)
        projected = dot(attended_s[rows].reshape(2 * tile_cols, width), w_out_s[...])
        level = (total_s[flat] + projected).astype(jnp.bfloat16)
        out_ref[rows] = level.reshape(2, tile_cols, width)
        return carry

    lax.fori_loop(0, tile_rows // 2, out_step, 0)

    for index, (sends, _, there, src, dst) in enumerate(moves):

        @pl.when(sends)
        def _():
            halo(index, there, src, dst).wait_send()

    others = pl.ds(1, n_device - 1)
    pltpu.make_async_copy(send_s.at[others], got_s.at[others], send_sem).wait()
    pltpu.make_async_copy(cell_send_s.at[others], cell_got_s.at[others], cell_send_sem).wait()


def local(image, skip_rows, owners, positions, gain, w_qkv, w_out, head_scale):
    tile_rows, tile_cols, width = image.shape
    n_device = lax.axis_size("row") * lax.axis_size("col")
    vmem = pl.BlockSpec(memory_space=pltpu.VMEM)
    smem = pl.BlockSpec(memory_space=pltpu.SMEM)
    far = pl.BlockSpec(memory_space=pl.ANY)
    rim = (CHUNKS, RIM, tile_cols // CHUNKS, width)
    side = (tile_rows * PAD, width)
    sides = (2 * tile_rows * PAD, width)
    extended = (tile_rows + 2 * RIM, tile_cols + 4 * PAD, width)
    n_query = GROUP_ROWS * GROUP_COLS * QUAD // HEAD
    n_key = (GROUP_ROWS + 2 * RIM) * (GROUP_COLS + 2 * PAD)
    bf16, f32 = jnp.bfloat16, jnp.float32
    n_chunk = n_device // 16
    n_move = 2 * CHUNKS + 6
    return pl.pallas_call(
        level_kernel,
        out_shape=jax.ShapeDtypeStruct(image.shape, bf16),
        in_specs=[vmem, vmem, vmem, smem, vmem, far, far, far],
        out_specs=vmem,
        scratch_shapes=[
            pltpu.VMEM((n_device, SLOTS, width), bf16),
            pltpu.VMEM((n_device, SLOTS, width), bf16),
            pltpu.VMEM((n_device, 1, 128), f32),
            pltpu.VMEM((n_device, 1, 128), f32),
            pltpu.VMEM((tile_rows * tile_cols, width), f32),
            pltpu.VMEM(image.shape, bf16),
            pltpu.VMEM(side, bf16),
            pltpu.VMEM(side, bf16),
            pltpu.VMEM(rim, bf16),
            pltpu.VMEM(rim, bf16),
            pltpu.VMEM(sides, bf16),
            pltpu.VMEM(sides, bf16),
            pltpu.VMEM(image.shape, bf16),
            pltpu.VMEM(w_qkv.shape, bf16),
            pltpu.VMEM(w_out.shape, bf16),
            pltpu.VMEM(image.shape, bf16),
            pltpu.VMEM(extended, f32),
            pltpu.VMEM(extended, f32),
            pltpu.VMEM(image.shape, bf16),
            pltpu.VMEM((tile_rows // GROUP_ROWS, width // QUAD, n_query, n_key), f32),
            pltpu.SemaphoreType.DMA,
            pltpu.SemaphoreType.DMA,
            pltpu.SemaphoreType.DMA((n_chunk,)),
            pltpu.SemaphoreType.DMA((n_chunk,)),
            pltpu.SemaphoreType.DMA((n_move,)),
            pltpu.SemaphoreType.DMA((n_move,)),
            pltpu.SemaphoreType.DMA((3,)),
            pltpu.SemaphoreType.REGULAR((2,)),
        ],
        compiler_params=pltpu.CompilerParams(
            collective_id=0, has_side_effects=True, vmem_limit_bytes=60 << 20
        ),
        name="level",
    )(
        skip_rows,
        owners.reshape(1, -1),
        positions.reshape(1, -1),
        head_scale,
        gain,
        image,
        w_qkv,
        w_out,
    )


def solution(mesh):
    in_specs = (
        P("row", "col", None),
        P(("row", "col"), None),
        P(("row", "col"), None),
        P(("row", "col")),
        P(),
        P(),
        P(),
        P(),
    )
    out_specs = P("row", "col", None)
    return jax.shard_map(local, mesh=mesh, in_specs=in_specs, out_specs=out_specs, check_vma=False)
```

```python
import functools

import jax
import jax.numpy as jnp
from jax import lax
from jax.experimental import pallas as pl
from jax.experimental.pallas import tpu as pltpu
from jax.sharding import PartitionSpec as P

RIM = 3
PAD = 4
CHUNKS = 4
GROUP_COLS = 16
HEAD = 64
QUAD = 256
SLOTS = 16
STRIDE = 49
STRIDE_INVERSE = 81
MESH = pl.DeviceIdType.MESH


def dot(a, b):
    return jnp.dot(a, b, preferred_element_type=jnp.float32)


def dot_nt(a, b):
    return lax.dot_general(a, b, (((1,), (1,)), ((), ())), preferred_element_type=jnp.float32)


def head_sums(x, ones):
    square = x * x
    high = square.astype(jnp.bfloat16)
    width = x.shape[1]
    parts = []
    for start in range(0, width, QUAD):
        lanes = slice(start, start + QUAD)
        parts.append(dot(high[:, lanes], ones))
    return jnp.concatenate(parts, axis=1)


def flag(condition):
    return jnp.where(condition, 1.0, 0.0).astype(jnp.bfloat16)


def coordinates(row, col):
    return col // 2, (col % 2) * 2 + (row // 2) % 2, row // 4, row % 2


def level_kernel(
    owner_ref, position_ref, scale_ref, gain_ref, rows_ref, image_ref, w_qkv_ref, w_out_ref,
    out_ref,
    send_s, got_s, cell_send_s, cell_got_s, total_s, own_s, left_s, right_s,
    up_land, down_land, left_land, right_land,
    rows_s, image_s, w_qkv_s, w_out_s, query_s, key_s, value_s, attended_s, score_s,
    send_sem, cell_send_sem, got_sems, cell_got_sems, halo_send_sems, halo_got_sems, load_sems, meet_sems,
):
    n_row, n_col = lax.axis_size("row"), lax.axis_size("col")
    n_device = n_row * n_col
    n_held, width = rows_ref.shape
    tile_rows, tile_cols, _ = image_ref.shape
    n_cell = tile_rows * tile_cols
    my_row, my_col = lax.axis_index("row"), lax.axis_index("col")
    my_x, my_y, my_z, my_core = coordinates(my_row, my_col)
    chunk = 16
    chunk_slots = chunk * SLOTS
    n_chunk = n_device // chunk

    def shifted(x_gap, y_gap, z_gap, core_gap):
        x, y, z = (my_x + x_gap) % 4, (my_y + y_gap) % 4, (my_z + z_gap) % 4
        core = (my_core + core_gap) % 2
        return (z * 4 + (y % 2) * 2 + core, x * 2 + y // 2)

    def partner(step):
        gap = (step * STRIDE) % n_device
        return shifted(gap // 32, (gap // 8) % 4, (gap // 2) % 4, gap % 2)

    x_peers = [(gap, 0, 0, 0) for gap in range(1, 4)]
    y_peers = [(0, gap, 0, 0) for gap in range(1, 4)]
    z_peers = [(0, 0, gap // 2, gap % 2) for gap in range(1, 8)]

    def signal(semaphore, peers):
        for peer in peers:
            pl.semaphore_signal(
                semaphore, inc=1, device_id=shifted(*peer), device_id_type=MESH
            )

    up_land[...] = jnp.zeros_like(up_land)
    down_land[...] = jnp.zeros_like(down_land)
    left_land[...] = jnp.zeros_like(left_land)
    right_land[...] = jnp.zeros_like(right_land)
    barrier = pltpu.get_barrier_semaphore()
    signal(barrier, x_peers + y_peers + z_peers)

    loads = [
        pltpu.make_async_copy(src, dst, load_sems.at[index])
        for index, (src, dst) in enumerate(
            (
                (image_ref, image_s),
                (w_qkv_ref, w_qkv_s),
                (w_out_ref, w_out_s),
                (rows_ref, rows_s),
            )
        )
    ]
    loads[3].start()
    loads[0].start()

    owner = owner_ref[...]
    owner_row, owner_col = owner >> 3, owner & 7
    gap_x = ((owner_col >> 1) - my_x) & 3
    gap_y = ((owner_col & 1) * 2 + ((owner_row >> 1) & 1) - my_y) & 3
    gap_z = ((owner_row >> 2) - my_z) & 3
    gap_core = ((owner_row & 1) - my_core) & 1
    order = ((((gap_x * 4 + gap_y) * 4 + gap_z) * 2 + gap_core) * STRIDE_INVERSE) & (n_device - 1)
    holds = lax.broadcasted_iota(jnp.int32, (n_device, n_held), 0) == order
    holds_f = jnp.where(holds, 1.0, 0.0)
    holds_b = holds_f.astype(jnp.bfloat16)
    earlier = jnp.zeros((n_device, n_held), jnp.float32)
    for start in range(0, n_held, 256):
        at = lax.broadcasted_iota(jnp.int32, (256, n_held), 0) + start
        to = lax.broadcasted_iota(jnp.int32, (256, n_held), 1)
        earlier = earlier + dot(holds_b[:, start : start + 256], flag(at < to))
    pl.semaphore_wait(barrier, len(x_peers + y_peers + z_peers))
    signal(meet_sems.at[0], y_peers)
    rank = jnp.sum(earlier * holds_f, axis=0, keepdims=True).astype(jnp.int32)
    slot = order * SLOTS + rank
    code = position_ref[...] + 1
    lane = lax.broadcasted_iota(jnp.int32, (128, n_held), 0)
    parts = jnp.where(lane == rank, (code >> 5).astype(jnp.float32), 0.0)
    parts = parts + jnp.where(lane == rank + SLOTS, (code & 31).astype(jnp.float32), 0.0)
    cell_send_s[...] = dot_nt(holds_b, parts.astype(jnp.bfloat16))[:, None, :]


    def row_copy(step):
        return pltpu.make_async_remote_copy(
            src_ref=send_s.at[step],
            dst_ref=got_s.at[step],
            send_sem=send_sem,
            recv_sem=got_sems.at[step // chunk],
            device_id=partner(step),
            device_id_type=MESH,
        )

    def cell_copy(step):
        return pltpu.make_async_remote_copy(
            src_ref=cell_send_s.at[step],
            dst_ref=cell_got_s.at[step],
            send_sem=cell_send_sem,
            recv_sem=cell_got_sems.at[step // chunk],
            device_id=partner(step),
            device_id_type=MESH,
        )

    def pack(index):
        at = lax.broadcasted_iota(jnp.int32, (chunk_slots, n_held), 0) + index * chunk_slots
        packed = dot(flag(at == slot), rows_s[...])
        send_s[pl.ds(index * chunk, chunk)] = packed.astype(jnp.bfloat16).reshape(
            chunk, SLOTS, width
        )

    def send(step, carry):
        cell_copy(step).start()
        row_copy(step).start()
        return carry

    pl.semaphore_wait(meet_sems.at[0], len(y_peers))
    signal(meet_sems.at[1], z_peers)
    loads[3].wait()
    pack(0)
    pl.semaphore_wait(meet_sems.at[1], len(z_peers))
    pltpu.make_async_copy(send_s.at[0], got_s.at[0], got_sems.at[0]).start()
    pltpu.make_async_copy(cell_send_s.at[0], cell_got_s.at[0], cell_got_sems.at[0]).start()
    lax.fori_loop(1, chunk, send, 0)

    def pack_step(index, carry):
        pack(index)
        lax.fori_loop(index * chunk, (index + 1) * chunk, send, 0)
        return carry

    lax.fori_loop(1, n_chunk, pack_step, 0)
    loads[0].wait()
    loads[1].start()
    loads[2].start()

    def fill_step(row, carry):
        total_s[row] = image_s[row].astype(jnp.float32)
        return carry

    lax.fori_loop(0, tile_rows, fill_step, 0)

    table_at = lax.broadcasted_iota(jnp.int32, (128, chunk_slots), 0)
    table_slot = lax.broadcasted_iota(jnp.int32, (128, chunk_slots), 1) % SLOTS
    table = jnp.where(table_at == table_slot, 32.0, 0.0)
    table = table + jnp.where(table_at == table_slot + SLOTS, 1.0, 0.0)
    table = table.astype(jnp.bfloat16)
    source_at = lax.broadcasted_iota(jnp.int32, (chunk, chunk_slots), 0)
    source_slot = lax.broadcasted_iota(jnp.int32, (chunk, chunk_slots), 1) // SLOTS

    def unpack_step(index, carry):
        blocks = pl.ds(index * chunk, chunk)
        pltpu.make_async_copy(
            cell_got_s.at[blocks], cell_got_s.at[blocks], cell_got_sems.at[index]
        ).wait()
        codes = dot(cell_got_s[blocks].reshape(chunk, 128).astype(jnp.bfloat16), table)
        code_row = jnp.sum(
            jnp.where(source_at == source_slot, codes, 0.0), axis=0, keepdims=True
        ).astype(jnp.int32)
        cell = lax.broadcasted_iota(jnp.int32, (n_cell, chunk_slots), 0) + 1
        chosen = flag(cell == code_row)
        pltpu.make_async_copy(got_s.at[blocks], got_s.at[blocks], got_sems.at[index]).wait()
        found = dot(chosen, got_s[blocks].reshape(chunk_slots, width))
        total_s[...] += found.reshape(tile_rows, tile_cols, width)
        return carry

    lax.fori_loop(0, n_chunk, unpack_step, 0)

    def norm(start, count):
        resid = total_s[start : start + count].reshape(count * tile_cols, width)
        mean = jnp.mean(resid * resid, axis=-1, keepdims=True)
        normed = resid * lax.rsqrt(mean + 1e-06) * gain_ref[...]
        own_s[start : start + count] = normed.astype(jnp.bfloat16).reshape(
            count, tile_cols, width
        )

    def halo(index, there, src, dst):
        return pltpu.make_async_remote_copy(
            src_ref=src,
            dst_ref=dst,
            send_sem=halo_send_sems.at[index],
            recv_sem=halo_got_sems.at[index],
            device_id=there,
            device_id_type=MESH,
        )

    has_up, has_down = my_row > 0, my_row < n_row - 1
    has_left, has_right = my_col > 0, my_col < n_col - 1
    above, below = my_row - 1, my_row + 1
    before, after = my_col - 1, my_col + 1
    side = tile_rows * PAD
    half = side // 2
    top, bottom = pl.ds(0, half), pl.ds(half, half)
    near_top, middle, near_bottom = pl.ds(0, half), pl.ds(half, side), pl.ds(half + side, half)
    moves = []
    part = tile_cols // 4
    bounds = (0, part, 2 * part, 3 * part, tile_cols)
    spans = [(bounds[index], bounds[index + 1] - bounds[index]) for index in range(CHUNKS)]
    for sends, gets, there, at, land in (
        (has_up, has_down, (above, my_col), 0, down_land),
        (has_down, has_up, (below, my_col), tile_rows - RIM, up_land),
    ):
        for index in range(CHUNKS):
            cols = pl.ds(*spans[index])
            moves.append(
                (sends, gets, there, own_s.at[pl.ds(at, RIM), cols], land.at[:, cols])
            )
    moves += [
        (has_left, has_right, (my_row, before), left_s, right_land.at[middle]),
        (has_right, has_left, (my_row, after), right_s, left_land.at[middle]),
        (
            has_up & has_left, has_down & has_right, (above, before),
            left_s.at[top], right_land.at[near_bottom],
        ),
        (
            has_up & has_right, has_down & has_left, (above, after),
            right_s.at[top], left_land.at[near_bottom],
        ),
        (
            has_down & has_left, has_up & has_right, (below, before),
            left_s.at[bottom], right_land.at[near_top],
        ),
        (
            has_down & has_right, has_up & has_left, (below, after),
            right_s.at[bottom], left_land.at[near_top],
        ),
    ]

    def start_move(index):
        sends, _, there, src, dst = moves[index]

        @pl.when(sends)
        def _():
            halo(index, there, src, dst).start()

    def end_move(index):
        _, gets, there, src, dst = moves[index]

        @pl.when(gets)
        def _():
            halo(index, there, src, dst).wait_recv()

    norm(0, RIM)
    start_move(0)
    start_move(1)
    norm(tile_rows - RIM, RIM)
    start_move(CHUNKS)
    start_move(CHUNKS + 1)
    norm(RIM, tile_rows - 2 * RIM)
    start_move(2)
    start_move(CHUNKS + 2)
    edge = 16
    pick_at = lax.broadcasted_iota(jnp.int32, (side, tile_rows * edge), 0)
    pick_from = lax.broadcasted_iota(jnp.int32, (side, tile_rows * edge), 1)
    pick_row, pick_col = pick_at // PAD, pick_at % PAD
    pick = flag((pick_from // edge == pick_row) & (pick_from % edge == pick_col))
    first = dot(pick, own_s[:, :edge].reshape(tile_rows * edge, width))
    left_s[...] = first.astype(jnp.bfloat16)
    pick_col = pick_col + edge - PAD
    pick = flag((pick_from // edge == pick_row) & (pick_from % edge == pick_col))
    last = dot(pick, own_s[:, tile_cols - edge :].reshape(tile_rows * edge, width))
    right_s[...] = last.astype(jnp.bfloat16)
    for index in range(2 * CHUNKS, len(moves)):
        start_move(index)
    for index in range(3, CHUNKS):
        start_move(index)
        start_move(CHUNKS + index)

    loads[1].wait()
    lane_a = lax.broadcasted_iota(jnp.int32, (QUAD, QUAD), 0) // HEAD
    lane_b = lax.broadcasted_iota(jnp.int32, (QUAD, QUAD), 1) // HEAD
    ones = flag(lane_a == lane_b)
    head_at = lax.broadcasted_iota(jnp.int32, (1, width), 1) // HEAD
    scale = jnp.zeros((1, width), jnp.float32)
    for head in range(width // HEAD):
        scale = jnp.where(head_at == head, scale_ref[head], scale)

    def keyval(x):
        keys = dot(x, w_qkv_s[:, width : 2 * width]).astype(jnp.bfloat16)
        keys = keys.astype(jnp.float32)
        unit = keys * lax.rsqrt(head_sums(keys, ones) + 1e-06)
        values = dot(x, w_qkv_s[:, 2 * width :])
        return unit, values

    own_cols = slice(PAD, PAD + tile_cols)
    batch = tile_rows // 2

    def own_step(step, carry):
        shape = (batch, tile_cols, width)
        x = own_s[pl.ds(step * batch, batch)].reshape(batch * tile_cols, width)
        unit, values = keyval(x)
        key_s[pl.ds(step * batch + RIM, batch), own_cols] = unit.reshape(shape)
        value_s[pl.ds(step * batch + RIM, batch), own_cols] = values.reshape(shape)
        queries = dot(x, w_qkv_s[:, :width])
        unit = queries * scale * lax.rsqrt(head_sums(queries, ones) + 1e-06)
        query_s[pl.ds(step * batch, batch)] = unit.astype(jnp.bfloat16).reshape(shape)
        return carry

    lax.fori_loop(0, tile_rows // batch, own_step, 0)

    def rim_step(index):
        end_move(index)
        end_move(CHUNKS + index)
        at_col, chunk_cols = spans[index]
        taken = slice(at_col, at_col + chunk_cols)
        n_rim = RIM * chunk_cols
        x = jnp.concatenate(
            [land[:, taken].reshape(n_rim, width) for land in (up_land, down_land)], axis=0
        )
        unit, values = keyval(x)
        shape = (RIM, chunk_cols, width)
        cols = slice(PAD + at_col, PAD + at_col + chunk_cols)
        for at, part in ((0, slice(0, n_rim)), (RIM + tile_rows, slice(n_rim, 2 * n_rim))):
            key_s[at : at + RIM, cols] = unit[part].reshape(shape)
            value_s[at : at + RIM, cols] = values[part].reshape(shape)

    def side_step():
        for index in range(2 * CHUNKS, len(moves)):
            end_move(index)
        n_side = 2 * side
        at = lax.broadcasted_iota(jnp.int32, (2 * n_side, 2 * n_side), 0)
        source = lax.broadcasted_iota(jnp.int32, (2 * n_side, 2 * n_side), 1)
        spot = at % (2 * PAD)
        wanted = (spot // PAD) * n_side + (at // (2 * PAD)) * PAD + spot % PAD
        x = jnp.concatenate([left_land[...], right_land[...]], axis=0)
        x = dot(flag(source == wanted), x).astype(jnp.bfloat16)
        unit, values = keyval(x)
        n_ext = tile_rows + 2 * RIM
        is_left = lax.broadcasted_iota(jnp.int32, (n_ext, 2 * PAD, width), 1) < PAD
        left_cols, right_cols = slice(0, 2 * PAD), slice(tile_cols, tile_cols + 2 * PAD)
        for ref, new in ((key_s, unit), (value_s, values)):
            new = new.reshape(2 * tile_rows, 2 * PAD, width)[1 : 1 + n_ext]
            ref[:, left_cols] = jnp.where(is_left, new, ref[:, left_cols])
            ref[:, right_cols] = jnp.where(is_left, ref[:, right_cols], new)

    image_rows, image_cols = tile_rows * n_row, tile_cols * n_col
    row_base, col_base = my_row * tile_rows, my_col * tile_cols
    key_cols = GROUP_COLS + 2 * PAD
    col_groups = tile_cols // GROUP_COLS
    lane_head = lax.broadcasted_iota(jnp.int32, (1, QUAD), 1) // HEAD
    heads = QUAD // HEAD
    masks = [flag(lane_head == head) for head in range(heads)]
    quads = range(0, width, QUAD)

    def shape_of(count):
        n_query, n_key = count * GROUP_COLS, (count + 2 * RIM) * key_cols
        query_at = lax.broadcasted_iota(jnp.int32, (n_query, n_key), 0)
        key_at = lax.broadcasted_iota(jnp.int32, (n_query, n_key), 1)
        key_row_at, key_col_at = key_at // key_cols, key_at % key_cols
        row_gap = key_row_at - query_at // GROUP_COLS
        col_gap = key_col_at - query_at % GROUP_COLS
        near = (
            (row_gap >= 0)
            & (row_gap <= 2 * RIM)
            & (col_gap >= PAD - RIM)
            & (col_gap <= PAD + RIM)
        )
        return n_query, n_key, key_row_at, key_col_at, near

    n_middle = tile_rows - 2 * RIM
    shapes = {RIM: shape_of(RIM), n_middle: shape_of(n_middle)}
    upper, middle_band, lower = (0, RIM), (RIM, n_middle), (tile_rows - RIM, RIM)

    def window(ref, band, col_at, lanes):
        start, count = band
        block = ref[start : start + count + 2 * RIM, pl.ds(col_at, key_cols), lanes]
        return block.reshape(-1, QUAD).astype(jnp.bfloat16)

    def column(group):
        return pl.multiple_of(group * GROUP_COLS, GROUP_COLS)

    def score(band, group, slot):
        start, count = band
        n_query, n_key, _, _, _ = shapes[count]
        col_at = column(group)
        for index, at in enumerate(quads):
            lanes = slice(at, at + QUAD)
            query = query_s[start : start + count, pl.ds(col_at, GROUP_COLS), lanes]
            query = query.reshape(n_query, QUAD)
            spread = jnp.concatenate([query * mask for mask in masks], axis=0)
            score_s[slot, index, : heads * n_query, :n_key] = dot_nt(
                spread, window(key_s, band, col_at, lanes)
            )

    def mix(band, group, slot):
        start, count = band
        n_query, n_key, key_row_at, key_col_at, near = shapes[count]
        col_at = column(group)
        key_row = row_base + start - RIM + key_row_at
        key_col = col_base + col_at - PAD + key_col_at
        inside = (
            near & (key_row >= 0) & (key_row < image_rows) & (key_col >= 0) & (key_col < image_cols)
        )
        bias = jnp.where(inside, 0.0, -1e30)
        for index, at in enumerate(quads):
            lanes = slice(at, at + QUAD)
            scores = score_s[slot, index, : heads * n_query, :n_key]
            scores = scores.reshape(heads, n_query, n_key) + bias[None]
            scores = scores.reshape(heads * n_query, n_key)
            top = jnp.max(scores, axis=1, keepdims=True)
            expo = jnp.exp(scores - top)
            inverse = 1.0 / jnp.sum(expo, axis=1, keepdims=True)
            mixed = dot(expo.astype(jnp.bfloat16), window(value_s, band, col_at, lanes))
            mixed = mixed * inverse
            joined = mixed[:n_query]
            for h in range(1, heads):
                part = mixed[h * n_query : (h + 1) * n_query]
                joined = jnp.where(lane_head == h, part, joined)
            attended_s[start : start + count, pl.ds(col_at, GROUP_COLS), lanes] = joined.astype(
                jnp.bfloat16
            ).reshape(count, GROUP_COLS, QUAD)

    def attend_middle(first, end):
        score(middle_band, first, 0)

        def step(index, carry):
            group = first + 2 * index
            score(middle_band, group + 1, 1)
            mix(middle_band, group, 0)
            score(middle_band, jnp.minimum(group + 2, col_groups - 1), 0)
            mix(middle_band, group + 1, 1)
            return carry

        lax.fori_loop(0, (end - first) // 2, step, 0)

    def attend(first, end):
        score(upper, first, 0)

        def step(group, carry):
            score(lower, group, 1)
            mix(upper, group, 0)
            score(upper, jnp.minimum(group + 1, col_groups - 1), 0)
            mix(lower, group, 1)
            return carry

        lax.fori_loop(first, end, step, 0)

    def project(first, end):
        cols = slice(first * GROUP_COLS, end * GROUP_COLS)
        flat = tile_rows * (end - first) * GROUP_COLS
        projected = dot(attended_s[:, cols].reshape(flat, width), w_out_s[...])
        level = total_s[:, cols] + projected.reshape(tile_rows, -1, width)
        out_ref[:, cols] = level.astype(jnp.bfloat16)

    attend_middle(1, col_groups - 1)
    rim_step(0)
    rim_step(1)
    attend(1, 3)
    rim_step(2)
    attend(3, 5)
    side_step()
    score(middle_band, 0, 0)
    score(middle_band, col_groups - 1, 1)
    mix(middle_band, 0, 0)
    mix(middle_band, col_groups - 1, 1)
    attend(0, 1)
    loads[2].wait()
    project(0, 5)
    rim_step(3)
    attend(5, col_groups)
    project(5, col_groups)

    for index, (sends, _, there, src, dst) in enumerate(moves):

        @pl.when(sends)
        def _():
            halo(index, there, src, dst).wait_send()

    others = pl.ds(1, n_device - 1)
    pltpu.make_async_copy(send_s.at[others], got_s.at[others], send_sem).wait()
    pltpu.make_async_copy(cell_send_s.at[others], cell_got_s.at[others], cell_send_sem).wait()


def local(image, skip_rows, owners, positions, gain, w_qkv, w_out, head_scale):
    tile_rows, tile_cols, width = image.shape
    n_device = lax.axis_size("row") * lax.axis_size("col")
    vmem = pl.BlockSpec(memory_space=pltpu.VMEM)
    smem = pl.BlockSpec(memory_space=pltpu.SMEM)
    far = pl.BlockSpec(memory_space=pl.ANY)
    rim = (RIM, tile_cols, width)
    side = (tile_rows * PAD, width)
    sides = (2 * tile_rows * PAD, width)
    extended = (tile_rows + 2 * RIM, tile_cols + 4 * PAD, width)
    n_query = RIM * GROUP_COLS * QUAD // HEAD
    n_key = 3 * RIM * (GROUP_COLS + 2 * PAD)
    bf16, f32 = jnp.bfloat16, jnp.float32
    n_chunk = n_device // 16
    n_move = 2 * CHUNKS + 6
    return pl.pallas_call(
        level_kernel,
        out_shape=jax.ShapeDtypeStruct(image.shape, bf16),
        in_specs=[vmem, vmem, smem, vmem, far, far, far, far],
        out_specs=vmem,
        scratch_shapes=[
            pltpu.VMEM((n_device, SLOTS, width), bf16),
            pltpu.VMEM((n_device, SLOTS, width), bf16),
            pltpu.VMEM((n_device, 1, 128), f32),
            pltpu.VMEM((n_device, 1, 128), f32),
            pltpu.VMEM(image.shape, f32),
            pltpu.VMEM(image.shape, bf16),
            pltpu.VMEM(side, bf16),
            pltpu.VMEM(side, bf16),
            pltpu.VMEM(rim, bf16),
            pltpu.VMEM(rim, bf16),
            pltpu.VMEM(sides, bf16),
            pltpu.VMEM(sides, bf16),
            pltpu.VMEM(skip_rows.shape, bf16),
            pltpu.VMEM(image.shape, bf16),
            pltpu.VMEM(w_qkv.shape, bf16),
            pltpu.VMEM(w_out.shape, bf16),
            pltpu.VMEM(image.shape, bf16),
            pltpu.VMEM(extended, f32),
            pltpu.VMEM(extended, f32),
            pltpu.VMEM(image.shape, bf16),
            pltpu.VMEM((2, width // QUAD, n_query, n_key), f32),
            pltpu.SemaphoreType.DMA,
            pltpu.SemaphoreType.DMA,
            pltpu.SemaphoreType.DMA((n_chunk,)),
            pltpu.SemaphoreType.DMA((n_chunk,)),
            pltpu.SemaphoreType.DMA((n_move,)),
            pltpu.SemaphoreType.DMA((n_move,)),
            pltpu.SemaphoreType.DMA((4,)),
            pltpu.SemaphoreType.REGULAR((2,)),
        ],
        compiler_params=pltpu.CompilerParams(
            collective_id=0, has_side_effects=True, vmem_limit_bytes=60 << 20
        ),
        name="level",
    )(
        owners.reshape(1, -1),
        positions.reshape(1, -1),
        head_scale,
        gain,
        skip_rows,
        image,
        w_qkv,
        w_out,
    )


def solution(mesh):
    in_specs = (
        P("row", "col", None),
        P(("row", "col"), None),
        P(("row", "col"), None),
        P(("row", "col")),
        P(),
        P(),
        P(),
        P(),
    )
    out_specs = P("row", "col", None)
    return jax.shard_map(local, mesh=mesh, in_specs=in_specs, out_specs=out_specs, check_vma=False)
```

```python
import functools

import jax
import jax.numpy as jnp
from jax import lax
from jax.experimental import pallas as pl
from jax.experimental.pallas import tpu as pltpu
from jax.sharding import PartitionSpec as P

RIM = 3
PAD = 4
CHUNKS = 4
GROUP_COLS = 16
HEAD = 64
QUAD = 256
SLOTS = 16
STRIDE = 49
STRIDE_INVERSE = 81
MESH = pl.DeviceIdType.MESH


def dot(a, b):
    return jnp.dot(a, b, preferred_element_type=jnp.float32)


def dot_nt(a, b):
    return lax.dot_general(a, b, (((1,), (1,)), ((), ())), preferred_element_type=jnp.float32)


def head_sums(x, ones):
    square = x * x
    high = square.astype(jnp.bfloat16)
    width = x.shape[1]
    parts = []
    for start in range(0, width, QUAD):
        lanes = slice(start, start + QUAD)
        parts.append(dot(high[:, lanes], ones))
    return jnp.concatenate(parts, axis=1)


def flag(condition):
    return jnp.where(condition, 1.0, 0.0).astype(jnp.bfloat16)


def coordinates(row, col):
    return col // 2, (col % 2) * 2 + (row // 2) % 2, row // 4, row % 2


def level_kernel(
    owner_ref, position_ref, scale_ref, gain_ref, rows_ref, image_ref, w_qkv_ref, w_out_ref,
    out_ref,
    send_s, got_s, cell_send_s, cell_got_s, total_s, own_s, left_s, right_s,
    up_land, down_land, left_land, right_land,
    rows_s, image_s, w_qkv_s, w_out_s, query_s, key_s, value_s, attended_s, score_s,
    send_sem, cell_send_sem, got_sems, cell_got_sems, halo_send_sems, halo_got_sems, load_sems, meet_sems,
):
    n_row, n_col = lax.axis_size("row"), lax.axis_size("col")
    n_device = n_row * n_col
    n_held, width = rows_ref.shape
    tile_rows, tile_cols, _ = image_ref.shape
    n_cell = tile_rows * tile_cols
    my_row, my_col = lax.axis_index("row"), lax.axis_index("col")
    my_x, my_y, my_z, my_core = coordinates(my_row, my_col)
    chunk = 16
    chunk_slots = chunk * SLOTS
    n_chunk = n_device // chunk

    def shifted(x_gap, y_gap, z_gap, core_gap):
        x, y, z = (my_x + x_gap) % 4, (my_y + y_gap) % 4, (my_z + z_gap) % 4
        core = (my_core + core_gap) % 2
        return (z * 4 + (y % 2) * 2 + core, x * 2 + y // 2)

    def partner(step):
        gap = (step * STRIDE) % n_device
        return shifted(gap // 32, (gap // 8) % 4, (gap // 2) % 4, gap % 2)

    x_peers = [(gap, 0, 0, 0) for gap in range(1, 4)]
    y_peers = [(0, gap, 0, 0) for gap in range(1, 4)]
    z_peers = [(0, 0, gap // 2, gap % 2) for gap in range(1, 8)]

    def signal(semaphore, peers):
        for peer in peers:
            pl.semaphore_signal(
                semaphore, inc=1, device_id=shifted(*peer), device_id_type=MESH
            )

    left_land[...] = jnp.zeros_like(left_land)
    right_land[...] = jnp.zeros_like(right_land)
    barrier = pltpu.get_barrier_semaphore()
    signal(barrier, x_peers + y_peers + z_peers)

    @pl.when(my_row == 0)
    def _():
        up_land[...] = jnp.zeros_like(up_land)

    @pl.when(my_row == n_row - 1)
    def _():
        down_land[...] = jnp.zeros_like(down_land)


    loads = [
        pltpu.make_async_copy(src, dst, load_sems.at[index])
        for index, (src, dst) in enumerate(
            (
                (image_ref, image_s),
                (w_qkv_ref, w_qkv_s),
                (w_out_ref, w_out_s),
                (rows_ref, rows_s),
            )
        )
    ]
    loads[3].start()
    loads[0].start()

    owner = owner_ref[...]
    owner_row, owner_col = owner >> 3, owner & 7
    gap_x = ((owner_col >> 1) - my_x) & 3
    gap_y = ((owner_col & 1) * 2 + ((owner_row >> 1) & 1) - my_y) & 3
    gap_z = ((owner_row >> 2) - my_z) & 3
    gap_core = ((owner_row & 1) - my_core) & 1
    order = ((((gap_x * 4 + gap_y) * 4 + gap_z) * 2 + gap_core) * STRIDE_INVERSE) & (n_device - 1)
    holds = lax.broadcasted_iota(jnp.int32, (n_device, n_held), 0) == order
    holds_f = jnp.where(holds, 1.0, 0.0)
    holds_b = holds_f.astype(jnp.bfloat16)
    earlier = jnp.zeros((n_device, n_held), jnp.float32)
    for start in range(0, n_held, 256):
        at = lax.broadcasted_iota(jnp.int32, (256, n_held), 0) + start
        to = lax.broadcasted_iota(jnp.int32, (256, n_held), 1)
        earlier = earlier + dot(holds_b[:, start : start + 256], flag(at < to))
    pl.semaphore_wait(barrier, len(x_peers + y_peers + z_peers))
    signal(meet_sems.at[0], y_peers)
    rank = jnp.sum(earlier * holds_f, axis=0, keepdims=True).astype(jnp.int32)
    slot = order * SLOTS + rank
    code = position_ref[...] + 1
    lane = lax.broadcasted_iota(jnp.int32, (128, n_held), 0)
    parts = jnp.where(lane == rank, (code >> 5).astype(jnp.float32), 0.0)
    parts = parts + jnp.where(lane == rank + SLOTS, (code & 31).astype(jnp.float32), 0.0)
    cell_send_s[...] = dot_nt(holds_b, parts.astype(jnp.bfloat16))[:, None, :]


    def row_copy(step):
        return pltpu.make_async_remote_copy(
            src_ref=send_s.at[step],
            dst_ref=got_s.at[step],
            send_sem=send_sem,
            recv_sem=got_sems.at[step // chunk],
            device_id=partner(step),
            device_id_type=MESH,
        )

    def cell_copy(step):
        return pltpu.make_async_remote_copy(
            src_ref=cell_send_s.at[step],
            dst_ref=cell_got_s.at[step],
            send_sem=cell_send_sem,
            recv_sem=cell_got_sems.at[step // chunk],
            device_id=partner(step),
            device_id_type=MESH,
        )

    def pack(index):
        at = lax.broadcasted_iota(jnp.int32, (chunk_slots, n_held), 0) + index * chunk_slots
        packed = dot(flag(at == slot), rows_s[...])
        send_s[pl.ds(index * chunk, chunk)] = packed.astype(jnp.bfloat16).reshape(
            chunk, SLOTS, width
        )

    def send(step, carry):
        cell_copy(step).start()
        row_copy(step).start()
        return carry

    pl.semaphore_wait(meet_sems.at[0], len(y_peers))
    signal(meet_sems.at[1], z_peers)
    loads[3].wait()
    pack(0)
    pl.semaphore_wait(meet_sems.at[1], len(z_peers))
    pltpu.make_async_copy(send_s.at[0], got_s.at[0], got_sems.at[0]).start()
    pltpu.make_async_copy(cell_send_s.at[0], cell_got_s.at[0], cell_got_sems.at[0]).start()
    lax.fori_loop(1, chunk, send, 0)

    def pack_step(index, carry):
        pack(index)
        lax.fori_loop(index * chunk, (index + 1) * chunk, send, 0)
        return carry

    lax.fori_loop(1, n_chunk, pack_step, 0)
    loads[0].wait()
    loads[1].start()
    loads[2].start()

    def fill_step(row, carry):
        total_s[row] = image_s[row].astype(jnp.float32)
        return carry

    lax.fori_loop(0, tile_rows, fill_step, 0)

    table_at = lax.broadcasted_iota(jnp.int32, (128, chunk_slots), 0)
    table_slot = lax.broadcasted_iota(jnp.int32, (128, chunk_slots), 1) % SLOTS
    table = jnp.where(table_at == table_slot, 32.0, 0.0)
    table = table + jnp.where(table_at == table_slot + SLOTS, 1.0, 0.0)
    table = table.astype(jnp.bfloat16)
    source_at = lax.broadcasted_iota(jnp.int32, (chunk, chunk_slots), 0)
    source_slot = lax.broadcasted_iota(jnp.int32, (chunk, chunk_slots), 1) // SLOTS

    def unpack_step(index, carry):
        blocks = pl.ds(index * chunk, chunk)
        pltpu.make_async_copy(
            cell_got_s.at[blocks], cell_got_s.at[blocks], cell_got_sems.at[index]
        ).wait()
        codes = dot(cell_got_s[blocks].reshape(chunk, 128).astype(jnp.bfloat16), table)
        code_row = jnp.sum(
            jnp.where(source_at == source_slot, codes, 0.0), axis=0, keepdims=True
        ).astype(jnp.int32)
        cell = lax.broadcasted_iota(jnp.int32, (n_cell, chunk_slots), 0) + 1
        chosen = flag(cell == code_row)
        pltpu.make_async_copy(got_s.at[blocks], got_s.at[blocks], got_sems.at[index]).wait()
        found = dot(chosen, got_s[blocks].reshape(chunk_slots, width))
        total_s[...] += found.reshape(tile_rows, tile_cols, width)
        return carry

    lax.fori_loop(0, n_chunk, unpack_step, 0)

    def norm(start, count):
        resid = total_s[start : start + count].reshape(count * tile_cols, width)
        mean = jnp.mean(resid * resid, axis=-1, keepdims=True)
        normed = resid * lax.rsqrt(mean + 1e-06) * gain_ref[...]
        own_s[start : start + count] = normed.astype(jnp.bfloat16).reshape(
            count, tile_cols, width
        )

    def halo(index, there, src, dst):
        return pltpu.make_async_remote_copy(
            src_ref=src,
            dst_ref=dst,
            send_sem=halo_send_sems.at[index],
            recv_sem=halo_got_sems.at[index],
            device_id=there,
            device_id_type=MESH,
        )

    has_up, has_down = my_row > 0, my_row < n_row - 1
    has_left, has_right = my_col > 0, my_col < n_col - 1
    above, below = my_row - 1, my_row + 1
    before, after = my_col - 1, my_col + 1
    side = tile_rows * PAD
    half = side // 2
    top, bottom = pl.ds(0, half), pl.ds(half, half)
    near_top, middle, near_bottom = pl.ds(0, half), pl.ds(half, side), pl.ds(half + side, half)
    moves = []
    part = tile_cols // 4
    bounds = (0, part, 2 * part, 3 * part, tile_cols)
    spans = [(bounds[index], bounds[index + 1] - bounds[index]) for index in range(CHUNKS)]
    for sends, gets, there, at, land in (
        (has_up, has_down, (above, my_col), 0, down_land),
        (has_down, has_up, (below, my_col), tile_rows - RIM, up_land),
    ):
        for index in range(CHUNKS):
            cols = pl.ds(*spans[index])
            moves.append(
                (sends, gets, there, own_s.at[pl.ds(at, RIM), cols], land.at[:, cols])
            )
    moves += [
        (has_left, has_right, (my_row, before), left_s, right_land.at[middle]),
        (has_right, has_left, (my_row, after), right_s, left_land.at[middle]),
        (
            has_up & has_left, has_down & has_right, (above, before),
            left_s.at[top], right_land.at[near_bottom],
        ),
        (
            has_up & has_right, has_down & has_left, (above, after),
            right_s.at[top], left_land.at[near_bottom],
        ),
        (
            has_down & has_left, has_up & has_right, (below, before),
            left_s.at[bottom], right_land.at[near_top],
        ),
        (
            has_down & has_right, has_up & has_left, (below, after),
            right_s.at[bottom], left_land.at[near_top],
        ),
    ]

    def start_move(index):
        sends, _, there, src, dst = moves[index]

        @pl.when(sends)
        def _():
            halo(index, there, src, dst).start()

    def end_move(index):
        _, gets, there, src, dst = moves[index]

        @pl.when(gets)
        def _():
            halo(index, there, src, dst).wait_recv()

    norm(0, RIM)
    start_move(0)
    start_move(1)
    norm(tile_rows - RIM, RIM)
    start_move(CHUNKS)
    start_move(CHUNKS + 1)
    norm(RIM, tile_rows - 2 * RIM)
    start_move(2)
    start_move(CHUNKS + 2)
    edge = 16
    pick_at = lax.broadcasted_iota(jnp.int32, (side, tile_rows * edge), 0)
    pick_from = lax.broadcasted_iota(jnp.int32, (side, tile_rows * edge), 1)
    pick_row, pick_col = pick_at // PAD, pick_at % PAD
    pick = flag((pick_from // edge == pick_row) & (pick_from % edge == pick_col))
    first = dot(pick, own_s[:, :edge].reshape(tile_rows * edge, width))
    left_s[...] = first.astype(jnp.bfloat16)
    pick_col = pick_col + edge - PAD
    pick = flag((pick_from // edge == pick_row) & (pick_from % edge == pick_col))
    last = dot(pick, own_s[:, tile_cols - edge :].reshape(tile_rows * edge, width))
    right_s[...] = last.astype(jnp.bfloat16)
    for index in range(2 * CHUNKS, len(moves)):
        start_move(index)
    for index in range(3, CHUNKS):
        start_move(index)
        start_move(CHUNKS + index)

    loads[1].wait()
    lane_a = lax.broadcasted_iota(jnp.int32, (QUAD, QUAD), 0) // HEAD
    lane_b = lax.broadcasted_iota(jnp.int32, (QUAD, QUAD), 1) // HEAD
    ones = flag(lane_a == lane_b)
    head_at = lax.broadcasted_iota(jnp.int32, (1, width), 1) // HEAD
    scale = jnp.zeros((1, width), jnp.float32)
    for head in range(width // HEAD):
        scale = jnp.where(head_at == head, scale_ref[head], scale)

    def keyval(x):
        keys = dot(x, w_qkv_s[:, width : 2 * width]).astype(jnp.bfloat16)
        keys = keys.astype(jnp.float32)
        unit = keys * lax.rsqrt(head_sums(keys, ones) + 1e-06)
        values = dot(x, w_qkv_s[:, 2 * width :])
        return unit, values

    own_cols = slice(PAD, PAD + tile_cols)
    batch = tile_rows // 2

    def own_step(step, carry):
        shape = (batch, tile_cols, width)
        x = own_s[pl.ds(step * batch, batch)].reshape(batch * tile_cols, width)
        unit, values = keyval(x)
        key_s[pl.ds(step * batch + RIM, batch), own_cols] = unit.reshape(shape)
        value_s[pl.ds(step * batch + RIM, batch), own_cols] = values.reshape(shape)
        queries = dot(x, w_qkv_s[:, :width])
        unit = queries * scale * lax.rsqrt(head_sums(queries, ones) + 1e-06)
        query_s[pl.ds(step * batch, batch)] = unit.astype(jnp.bfloat16).reshape(shape)
        return carry

    lax.fori_loop(0, tile_rows // batch, own_step, 0)

    def rim_step(index):
        end_move(index)
        end_move(CHUNKS + index)
        at_col, chunk_cols = spans[index]
        taken = slice(at_col, at_col + chunk_cols)
        n_rim = RIM * chunk_cols
        x = jnp.concatenate(
            [land[:, taken].reshape(n_rim, width) for land in (up_land, down_land)], axis=0
        )
        unit, values = keyval(x)
        shape = (RIM, chunk_cols, width)
        cols = slice(PAD + at_col, PAD + at_col + chunk_cols)
        for at, part in ((0, slice(0, n_rim)), (RIM + tile_rows, slice(n_rim, 2 * n_rim))):
            key_s[at : at + RIM, cols] = unit[part].reshape(shape)
            value_s[at : at + RIM, cols] = values[part].reshape(shape)

    def side_step():
        for index in range(2 * CHUNKS, len(moves)):
            end_move(index)
        n_side = 2 * side
        at = lax.broadcasted_iota(jnp.int32, (2 * n_side, 2 * n_side), 0)
        source = lax.broadcasted_iota(jnp.int32, (2 * n_side, 2 * n_side), 1)
        spot = at % (2 * PAD)
        wanted = (spot // PAD) * n_side + (at // (2 * PAD)) * PAD + spot % PAD
        x = jnp.concatenate([left_land[...], right_land[...]], axis=0)
        x = dot(flag(source == wanted), x).astype(jnp.bfloat16)
        unit, values = keyval(x)
        n_ext = tile_rows + 2 * RIM
        is_left = lax.broadcasted_iota(jnp.int32, (n_ext, 2 * PAD, width), 1) < PAD
        left_cols, right_cols = slice(0, 2 * PAD), slice(tile_cols, tile_cols + 2 * PAD)
        for ref, new in ((key_s, unit), (value_s, values)):
            new = new.reshape(2 * tile_rows, 2 * PAD, width)[1 : 1 + n_ext]
            ref[:, left_cols] = jnp.where(is_left, new, ref[:, left_cols])
            ref[:, right_cols] = jnp.where(is_left, ref[:, right_cols], new)

    image_rows, image_cols = tile_rows * n_row, tile_cols * n_col
    row_base, col_base = my_row * tile_rows, my_col * tile_cols
    key_cols = GROUP_COLS + 2 * PAD
    col_groups = tile_cols // GROUP_COLS
    lane_head = lax.broadcasted_iota(jnp.int32, (1, QUAD), 1) // HEAD
    heads = QUAD // HEAD
    masks = [flag(lane_head == head) for head in range(heads)]
    quads = range(0, width, QUAD)

    def shape_of(count):
        n_query, n_key = count * GROUP_COLS, (count + 2 * RIM) * key_cols
        query_at = lax.broadcasted_iota(jnp.int32, (n_query, n_key), 0)
        key_at = lax.broadcasted_iota(jnp.int32, (n_query, n_key), 1)
        key_row_at, key_col_at = key_at // key_cols, key_at % key_cols
        row_gap = key_row_at - query_at // GROUP_COLS
        col_gap = key_col_at - query_at % GROUP_COLS
        near = (
            (row_gap >= 0)
            & (row_gap <= 2 * RIM)
            & (col_gap >= PAD - RIM)
            & (col_gap <= PAD + RIM)
        )
        return n_query, n_key, key_row_at, key_col_at, near

    n_middle = tile_rows - 2 * RIM
    shapes = {RIM: shape_of(RIM), n_middle: shape_of(n_middle)}
    upper, middle_band, lower = (0, RIM), (RIM, n_middle), (tile_rows - RIM, RIM)

    def window(ref, band, col_at, lanes):
        start, count = band
        block = ref[start : start + count + 2 * RIM, pl.ds(col_at, key_cols), lanes]
        return block.reshape(-1, QUAD).astype(jnp.bfloat16)

    def column(group):
        return pl.multiple_of(group * GROUP_COLS, GROUP_COLS)

    def score(band, group, slot):
        start, count = band
        n_query, n_key, _, _, _ = shapes[count]
        col_at = column(group)
        for index, at in enumerate(quads):
            lanes = slice(at, at + QUAD)
            query = query_s[start : start + count, pl.ds(col_at, GROUP_COLS), lanes]
            query = query.reshape(n_query, QUAD)
            spread = jnp.concatenate([query * mask for mask in masks], axis=0)
            score_s[slot, index, : heads * n_query, :n_key] = dot_nt(
                spread, window(key_s, band, col_at, lanes)
            )

    def mix(band, group, slot):
        start, count = band
        n_query, n_key, key_row_at, key_col_at, near = shapes[count]
        col_at = column(group)
        key_row = row_base + start - RIM + key_row_at
        key_col = col_base + col_at - PAD + key_col_at
        inside = (
            near & (key_row >= 0) & (key_row < image_rows) & (key_col >= 0) & (key_col < image_cols)
        )
        bias = jnp.where(inside, 0.0, -1e30)
        for index, at in enumerate(quads):
            lanes = slice(at, at + QUAD)
            scores = score_s[slot, index, : heads * n_query, :n_key]
            scores = scores.reshape(heads, n_query, n_key) + bias[None]
            scores = scores.reshape(heads * n_query, n_key)
            top = jnp.max(scores, axis=1, keepdims=True)
            expo = jnp.exp(scores - top)
            inverse = 1.0 / jnp.sum(expo, axis=1, keepdims=True)
            mixed = dot(expo.astype(jnp.bfloat16), window(value_s, band, col_at, lanes))
            mixed = mixed * inverse
            joined = mixed[:n_query]
            for h in range(1, heads):
                part = mixed[h * n_query : (h + 1) * n_query]
                joined = jnp.where(lane_head == h, part, joined)
            attended_s[start : start + count, pl.ds(col_at, GROUP_COLS), lanes] = joined.astype(
                jnp.bfloat16
            ).reshape(count, GROUP_COLS, QUAD)

    def attend_middle(first, end):
        score(middle_band, first, 0)

        def step(index, carry):
            group = first + 2 * index
            score(middle_band, group + 1, 1)
            mix(middle_band, group, 0)
            score(middle_band, jnp.minimum(group + 2, col_groups - 1), 0)
            mix(middle_band, group + 1, 1)
            return carry

        lax.fori_loop(0, (end - first) // 2, step, 0)

    def attend(first, end):
        score(upper, first, 0)

        def step(group, carry):
            score(lower, group, 1)
            mix(upper, group, 0)
            score(upper, jnp.minimum(group + 1, col_groups - 1), 0)
            mix(lower, group, 1)
            return carry

        lax.fori_loop(first, end, step, 0)

    def project(first, end):
        cols = slice(first * GROUP_COLS, end * GROUP_COLS)
        flat = tile_rows * (end - first) * GROUP_COLS
        projected = dot(attended_s[:, cols].reshape(flat, width), w_out_s[...])
        level = total_s[:, cols] + projected.reshape(tile_rows, -1, width)
        out_ref[:, cols] = level.astype(jnp.bfloat16)

    attend_middle(1, col_groups - 1)
    rim_step(0)
    rim_step(1)
    attend(1, 3)
    rim_step(2)
    attend(3, 5)
    side_step()
    score(middle_band, 0, 0)
    score(middle_band, col_groups - 1, 1)
    mix(middle_band, 0, 0)
    mix(middle_band, col_groups - 1, 1)
    attend(0, 1)
    loads[2].wait()
    project(0, 5)
    rim_step(3)
    attend(5, col_groups)
    project(5, col_groups)

    for index, (sends, _, there, src, dst) in enumerate(moves):

        @pl.when(sends)
        def _():
            halo(index, there, src, dst).wait_send()

    others = pl.ds(1, n_device - 1)
    pltpu.make_async_copy(send_s.at[others], got_s.at[others], send_sem).wait()
    pltpu.make_async_copy(cell_send_s.at[others], cell_got_s.at[others], cell_send_sem).wait()


def local(image, skip_rows, owners, positions, gain, w_qkv, w_out, head_scale):
    tile_rows, tile_cols, width = image.shape
    n_device = lax.axis_size("row") * lax.axis_size("col")
    vmem = pl.BlockSpec(memory_space=pltpu.VMEM)
    smem = pl.BlockSpec(memory_space=pltpu.SMEM)
    far = pl.BlockSpec(memory_space=pl.ANY)
    rim = (RIM, tile_cols, width)
    side = (tile_rows * PAD, width)
    sides = (2 * tile_rows * PAD, width)
    extended = (tile_rows + 2 * RIM, tile_cols + 4 * PAD, width)
    n_query = RIM * GROUP_COLS * QUAD // HEAD
    n_key = 3 * RIM * (GROUP_COLS + 2 * PAD)
    bf16, f32 = jnp.bfloat16, jnp.float32
    n_chunk = n_device // 16
    n_move = 2 * CHUNKS + 6
    return pl.pallas_call(
        level_kernel,
        out_shape=jax.ShapeDtypeStruct(image.shape, bf16),
        in_specs=[vmem, vmem, smem, vmem, far, far, far, far],
        out_specs=vmem,
        scratch_shapes=[
            pltpu.VMEM((n_device, SLOTS, width), bf16),
            pltpu.VMEM((n_device, SLOTS, width), bf16),
            pltpu.VMEM((n_device, 1, 128), f32),
            pltpu.VMEM((n_device, 1, 128), f32),
            pltpu.VMEM(image.shape, f32),
            pltpu.VMEM(image.shape, bf16),
            pltpu.VMEM(side, bf16),
            pltpu.VMEM(side, bf16),
            pltpu.VMEM(rim, bf16),
            pltpu.VMEM(rim, bf16),
            pltpu.VMEM(sides, bf16),
            pltpu.VMEM(sides, bf16),
            pltpu.VMEM(skip_rows.shape, bf16),
            pltpu.VMEM(image.shape, bf16),
            pltpu.VMEM(w_qkv.shape, bf16),
            pltpu.VMEM(w_out.shape, bf16),
            pltpu.VMEM(image.shape, bf16),
            pltpu.VMEM(extended, f32),
            pltpu.VMEM(extended, f32),
            pltpu.VMEM(image.shape, bf16),
            pltpu.VMEM((2, width // QUAD, n_query, n_key), f32),
            pltpu.SemaphoreType.DMA,
            pltpu.SemaphoreType.DMA,
            pltpu.SemaphoreType.DMA((n_chunk,)),
            pltpu.SemaphoreType.DMA((n_chunk,)),
            pltpu.SemaphoreType.DMA((n_move,)),
            pltpu.SemaphoreType.DMA((n_move,)),
            pltpu.SemaphoreType.DMA((4,)),
            pltpu.SemaphoreType.REGULAR((2,)),
        ],
        compiler_params=pltpu.CompilerParams(
            collective_id=0, has_side_effects=True, vmem_limit_bytes=60 << 20
        ),
        name="level",
    )(
        owners.reshape(1, -1),
        positions.reshape(1, -1),
        head_scale,
        gain,
        skip_rows,
        image,
        w_qkv,
        w_out,
    )


def solution(mesh):
    in_specs = (
        P("row", "col", None),
        P(("row", "col"), None),
        P(("row", "col"), None),
        P(("row", "col")),
        P(),
        P(),
        P(),
        P(),
    )
    out_specs = P("row", "col", None)
    return jax.shard_map(local, mesh=mesh, in_specs=in_specs, out_specs=out_specs, check_vma=False)
```
